32 devices in a mesh: dp: 4 (over x, core), expert: 8 (over z, y).
Axes of the slice: x: 2, y: 2, z: 4, core: 2. Of those that a mesh axis runs over, the one named last changes fastest.
Arguments:
- tokens: bfloat16 [4096, 768], P(('dp', 'expert')), may hold values from -6 to 6
- attn_weights: bfloat16 [3072, 768], P(('dp', 'expert')), may hold values from -0.3125 to 0.3125
- gain_attn: float32 [768], replicated, may hold values from 0.5 to 1.5
- gain_ffn: float32 [768], replicated, may hold values from 0.5 to 1.5
- rel_table: float32 [32, 12], replicated, may hold values from -4 to 4
- expert_in: bfloat16 [8, 768, 3072], P('expert', None, 'dp'), may hold values from -0.21875 to 0.21875
- expert_out: bfloat16 [8, 3072, 768], P('expert', 'dp'), may hold values from -0.21875 to 0.21875
- gate_weights: float32 [4096, 2], P(('dp', 'expert')), may hold values from 0.25 to 0.75
- expert_ids: int32 [4096, 2], P(('dp', 'expert')), may hold values from 0 to 7, all different within a row; in each aligned block of 64 rows (0 to 63, 64 to 127, ...) at most 24 rows name the same one
- doc_ids: int32 [64, 64], P(('dp', 'expert')), may hold values from 0 to 3, never falling along the last dimension, each value on 1 to 32 neighbouring positions
- cotangent: bfloat16 [4096, 768], P(('dp', 'expert')), may hold values from -6 to 6
Outputs:
- output: bfloat16 [4096, 768], P(('dp', 'expert'))
- grad_tokens: float32 [4096, 768], P(('dp', 'expert'))
- grad_attn_weights: float32 [3072, 768], P(('dp', 'expert'))
- grad_gain_attn: float32 [768], replicated
- grad_gain_ffn: float32 [768], replicated
- grad_rel_table: float32 [32, 12], replicated
- grad_expert_in: float32 [8, 768, 3072], P('expert', None, 'dp')
- grad_expert_out: float32 [8, 3072, 768], P('expert', 'dp')
The draws below stay inside these ranges and needn't reach their ends.
Inputs may be any that keep to these rules, and one draw needn't show every extreme that they name: `expert_ids`: the two experts of a token differ. Within each aligned block of 64 tokens (one micro-batch of one device) no expert is named more than 24 times; in some blocks some expert exactly 24 times. `doc_ids`: within each sequence the numbers never fall; each of the four documents holds 1 to half of 64 tokens, and one exactly half.
All inputs are finite; a program needn't handle non-finite values.
Results may differ from the reference program's by a relative error of at most 0.012.
The reference program's roundings to bfloat16 on the way count: a program that leaves them out, or rounds other values in their place, can miss the bound.
Values may be sent and summed in bfloat16 or wider, within the bound.
No kernel may reach another device: no remote copies, remote signals or barrier semaphores. Data moves between devices by JAX's collectives and lax.ppermute only.
A program may use at most 128 MiB of HBM per device.

```python
import math
import jax
import jax.numpy as jnp
import numpy as np
from jax import lax

D = 768
HEADS = 12
HD = 64
FF = 3072
BUCKETS = 32
TOK_MB = 64
SEQ = 64
EXPERTS = 8
CAP = 24
TOKENS = 4096
SEQS = 64


def steps_of(key, extent, split, smallest, top_value):
    loudness = 1.0
    for axis_at, shards_of in split:
        steps = jax.random.uniform(jax.random.fold_in(jax.random.fold_in(key, 6), axis_at), (shards_of,), jnp.float32, smallest / len(split), top_value / len(split))
        loudness = loudness * jnp.repeat(jnp.exp(steps), extent[axis_at] // shards_of).reshape((-1,) + (1,) * (len(extent) - 1 - axis_at))
    return loudness


def split_up(amount, total, most, lean):
    portions = [(1 << 20) // math.isqrt(standing ** lean) + 1 for standing in range(2, amount + 1)]
    surplus, given = total - most - (amount - 1), [1] * (amount - 1)
    while surplus > 0:
        free = [i for i in range(amount - 1) if given[i] < most]
        whole, left = sum([portions[i] for i in free]), surplus
        for i in free:
            extra = min(most - given[i], max(1, left * portions[i] // whole), surplus)
            given[i] = given[i] + extra
            surplus = surplus - extra
    return np.array([most] + given)


def uneven(rng, count, total, bound, lean):
    if count == 2:
        one = jax.random.randint(rng, (), max(1, total - bound), min(bound, total - 1) + 1)
        return jnp.stack([one, total - one])
    sizes = jnp.asarray(split_up(count, total, bound, lean), jnp.int32)
    couples = (count - 1) // 2
    donor, receiver = sizes[1:1 + 2 * couples:2], sizes[2:2 + 2 * couples:2]
    margin = jnp.minimum(donor - 1, bound - receiver)
    passed = jax.random.randint(jax.random.fold_in(rng, 1), (couples,), 0, 1 << 20) % (margin + 1)
    sizes = sizes.at[1:1 + 2 * couples:2].set(donor - passed).at[2:2 + 2 * couples:2].set(receiver + passed)
    return sizes[jax.random.permutation(jax.random.fold_in(rng, 2), count)]


def shared_out(stream_key, own, number, rows, amount, top, limit, skew):
    ranking = jax.random.permutation(stream_key, amount)
    crowded, common = portions_of(amount, rows * top, limit, skew, True), portions_of(amount, rows * top, limit, skew, False)
    places = jnp.arange(amount)

    def named(tallies, turn):
        used = int((tallies > 0).sum())
        fixed = max(1, used // 4)
        moved = fixed + (places - fixed + turn * (used - fixed)) % max(1, amount - fixed)
        return jnp.zeros((amount,), jnp.int32).at[ranking[jnp.where(places < fixed, places, moved)]].set(jnp.asarray(tallies, jnp.int32))

    tallies = jnp.where(number % 4 == 0, named(crowded, number // 4), named(common, number - number // 4 - 1))
    mixed = jax.random.permutation(jax.random.fold_in(own, 3), amount)
    donor, taker = mixed[0:amount // 2 * 2:2], mixed[1:amount // 2 * 2:2]
    margin = jnp.minimum(tallies[donor] - 1, limit - tallies[taker]) // 2
    margin = jnp.where((donor == ranking[0]) | (taker == ranking[0]) | (tallies[taker] == 0), 0, jnp.maximum(margin, 0))
    moved = jax.random.randint(jax.random.fold_in(own, 4), (amount // 2,), 0, 1 << 20) % (margin + 1)
    tallies = tallies.at[donor].add(-moved).at[taker].add(moved)
    labels = jnp.searchsorted(jnp.cumsum(tallies), jnp.arange(rows * top), side="right").astype(jnp.int32)
    grid = labels.reshape(top, rows).T
    grid = grid[jax.random.permutation(jax.random.fold_in(own, 1), rows)]
    turn = jax.random.randint(jax.random.fold_in(own, 2), (rows, 1), 0, top)
    return jnp.take_along_axis(grid, (jnp.arange(top)[None, :] + turn) % top, axis=1)


def portions_of(amount, total, reach, lean, full):
    portions = [(1 << 20) // math.isqrt(standing ** lean) + 1 for standing in range(1, amount + 1)]
    largest = reach if full else min(reach, max(-(-total // amount), total * portions[0] // sum(portions)))
    least = 1 if total - largest >= amount - 1 else 0
    holding, spare = [largest] + [least] * (amount - 1), total - largest - least * (amount - 1)
    while spare > 0:
        free = [i for i in range(1, amount) if holding[i] < largest] or [i for i in range(1, amount) if holding[i] < reach]
        pool, left = sum([portions[i] for i in free]), spare
        for i in free:
            more = min(reach - holding[i], max(1, left * portions[i] // pool), spare)
            holding[i] = holding[i] + more
            spare = spare - more
    return np.array(holding)


def scatter_about(own_key, dims, width, reach, cuts=(), kind=jnp.bfloat16):
    loudness = steps_of(own_key, dims, cuts, -0.22, 0.18) if cuts else 1.0
    entries = jax.random.normal(own_key, dims, jnp.float32) * width * loudness
    return jnp.minimum(jnp.maximum(entries, -reach), reach).astype(kind)


def setup_inputs(seed: int = 0) -> dict:
    key_of = jax.random.split(jax.random.key(seed), 12)
    tokens = scatter_about(key_of[0], (TOKENS, D), 1.0, 6.0, ((0, 32),))
    attn_weights = scatter_about(key_of[1], (4 * D, D), (D // 2) ** -0.5, 0.3125, ((0, 32),))
    gain_attn = jnp.clip(1.0 + 0.1 * jax.random.normal(key_of[2], (D,), jnp.float32), 0.5, 1.5)
    gain_ffn = jnp.clip(1.0 + 0.1 * jax.random.normal(key_of[3], (D,), jnp.float32), 0.5, 1.5)
    rel_table = scatter_about(key_of[4], (BUCKETS, HEADS), 1.0, 4.0, (), jnp.float32)
    expert_in = scatter_about(key_of[5], (EXPERTS, D, FF), D ** -0.5, 0.21875, ((0, 8), (2, 4)))
    expert_out = scatter_about(key_of[6], (EXPERTS, FF, D), (FF // 4) ** -0.5, 0.21875, ((0, 8), (1, 4)))
    gate_weights = jnp.clip(0.25 + 0.5 * jax.random.uniform(key_of[7], (TOKENS, 2), jnp.float32) ** steps_of(key_of[7], (TOKENS, 2), ((0, 32),), -0.2, 0.2), 0.25, 0.75)
    expert_ids_keys = jax.random.split(jax.random.fold_in(key_of[8], 1), TOKENS // TOK_MB)
    expert_ids_turns = jax.random.permutation(jax.random.fold_in(key_of[8], 3), TOKENS // TOK_MB)
    expert_ids = jax.vmap(lambda own, number: shared_out(jax.random.fold_in(key_of[8], 2), own, number, TOK_MB, EXPERTS, 2, CAP, 1))(expert_ids_keys, expert_ids_turns).reshape((TOKENS, 2))
    doc_ids = jax.vmap(lambda own: jnp.searchsorted(jnp.cumsum(uneven(own, 4, SEQ, SEQ // 2, 0)), jnp.arange(SEQ), side="right"))(jax.random.split(key_of[9], SEQS)).reshape((SEQS, SEQ)).astype(jnp.int32)
    cotangent = scatter_about(key_of[10], (TOKENS, D), 1.0, 6.0, ((0, 32),))
    return {"tokens": tokens, "attn_weights": attn_weights, "gain_attn": gain_attn, "gain_ffn": gain_ffn, "rel_table": rel_table, "expert_in": expert_in, "expert_out": expert_out, "gate_weights": gate_weights, "expert_ids": expert_ids, "doc_ids": doc_ids, "cotangent": cotangent}


epsilon = 1e-06
top_precision = lax.Precision.HIGHEST

@jax.custom_vjp
def low(v):
    return lax.optimization_barrier(v.astype(jnp.bfloat16)).astype(jnp.float32)

@jax.custom_vjp
def low_back(v):
    return v

def low_keep(v):
    return (low(v), None)

def low_pass(kept, grad):
    return (grad,)

def back_keep(v):
    return (v, None)

def back_low(kept, grad):
    return (low(grad),)
low.defvjp(low_keep, low_pass)
low_back.defvjp(back_keep, back_low)

def bucket_table(length, top_bucket):
    offset = np.arange(length)[:, None] - np.arange(length)[None, :]
    offset = np.maximum(offset, 0)
    octave = offset * 0
    for exponent in range(1, 24):
        octave = octave + (offset >= 2 ** exponent)
    shifted = offset >> np.maximum(octave - 2, 0)
    logbucket = 16 + 4 * (octave - 4) + (shifted & 3)
    return np.where(offset < 16, offset, np.minimum(logbucket, top_bucket))

def rms_norm(values, gain_vec):
    return values * lax.rsqrt(lax.optimization_barrier(jnp.mean(values * values, axis=-1, keepdims=True)) + epsilon) * gain_vec

def attend(query_rows, key_rows, value_rows, rel_bias, allowed):
    scores = jnp.einsum('gqhd,gkhd->ghqk', query_rows, key_rows, precision=top_precision, preferred_element_type=jnp.float32)
    scores = low_back(scores * 0.125 + rel_bias[None])
    scores = jnp.where(allowed[:, None, :, :], scores, -1000000000.0)
    attn_probs = low(jax.nn.softmax(scores, axis=-1))
    return jnp.einsum('ghqk,gkhd->gqhd', attn_probs, value_rows, precision=top_precision, preferred_element_type=jnp.float32)

def expert_ffn(slot_rows, w_first, w_second):
    pre_act = low_back(jnp.dot(slot_rows, w_first, precision=top_precision, preferred_element_type=jnp.float32))
    hidden = low(jax.nn.gelu(pre_act, approximate=True))
    return low_back(low(jnp.dot(hidden, w_second, precision=top_precision, preferred_element_type=jnp.float32)))

def forward(tokens, attn_weights, gain_attn, gain_ffn, rel_table, expert_in, expert_out, gate_weights, positions, allowed, bucket_ids):
    rows_each = TOKENS // TOK_MB * CAP
    normed = low(rms_norm(tokens, gain_attn))
    w_query = attn_weights[0:D]
    w_key = attn_weights[D:2 * D]
    w_value = attn_weights[2 * D:3 * D]
    w_output = attn_weights[3 * D:4 * D]
    query_rows = low_back(low(jnp.dot(normed, w_query, precision=top_precision, preferred_element_type=jnp.float32)))
    key_rows = low_back(low(jnp.dot(normed, w_key, precision=top_precision, preferred_element_type=jnp.float32)))
    value_rows = low_back(low(jnp.dot(normed, w_value, precision=top_precision, preferred_element_type=jnp.float32)))
    group_size = math.gcd(SEQS, max(1, 4096 // SEQ))
    group_shape = (SEQS // group_size, group_size, SEQ, HEADS, HD)
    rel_bias = jnp.transpose(rel_table[bucket_ids], (2, 0, 1))

    def attend_group(items):
        return attend(items[0], items[1], items[2], rel_bias, items[3])
    mixed = lax.map(jax.checkpoint(attend_group), (query_rows.reshape(group_shape), key_rows.reshape(group_shape), value_rows.reshape(group_shape), allowed.reshape(SEQS // group_size, group_size, SEQ, SEQ)))
    mixed_rows = low_back(low(mixed.reshape(TOKENS, D)))
    attn_out = low_back(jnp.dot(mixed_rows, w_output, precision=top_precision, preferred_element_type=jnp.float32))
    residual = tokens + attn_out
    moe_in = low(rms_norm(residual, gain_ffn))
    buffer = jnp.zeros((EXPERTS * rows_each, D), jnp.float32).at[positions.reshape(-1)].set(jnp.repeat(moe_in, 2, axis=0))
    buffer = low_back(buffer)

    def expert_group(items):
        return expert_ffn(items[0], items[1], items[2])
    results = lax.map(jax.checkpoint(expert_group), (buffer.reshape(EXPERTS, rows_each, D), expert_in, expert_out))
    picked = results.reshape(EXPERTS * rows_each, D)[positions]
    moe_out = lax.optimization_barrier(jnp.sum(gate_weights[:, :, None] * picked, axis=1))
    return residual + moe_out

def reference(tokens, attn_weights, gain_attn, gain_ffn, rel_table, expert_in, expert_out, gate_weights, expert_ids, doc_ids, cotangent):
    block_count = TOKENS // TOK_MB
    rows_each = block_count * CAP
    id_blocks = expert_ids.reshape(block_count, 2 * TOK_MB).astype(jnp.int32)
    onehot = (id_blocks[:, :, None] == jnp.arange(EXPERTS, dtype=jnp.int32)[None, None, :]).astype(jnp.int32)
    slot_index = lax.optimization_barrier(jnp.sum(jnp.cumsum(onehot, axis=1) * onehot, axis=2)) - 1
    block_base = (jnp.arange(block_count, dtype=jnp.int32) * CAP)[:, None]
    positions = (id_blocks * rows_each + block_base + slot_index).reshape(TOKENS, 2).astype(jnp.int32)
    causal = jnp.asarray(np.tril(np.ones((SEQ, SEQ), dtype=np.int32)) > 0)
    allowed = (doc_ids[:, :, None] == doc_ids[:, None, :]) & causal[None]
    bucket_ids = jnp.asarray(bucket_table(SEQ, BUCKETS - 1).astype(np.int32))

    def run(tok_float, attn_float, gain_one, gain_two, table_float, first_float, second_float):
        return forward(tok_float, attn_float, gain_one, gain_two, table_float, first_float, second_float, gate_weights, positions, allowed, bucket_ids)
    output, pullback = jax.vjp(run, tokens.astype(jnp.float32), attn_weights.astype(jnp.float32), gain_attn, gain_ffn, rel_table, expert_in.astype(jnp.float32), expert_out.astype(jnp.float32))
    gradients = pullback(cotangent.astype(jnp.float32))
    return (output.astype(jnp.bfloat16), gradients[0], gradients[1], gradients[2], gradients[3], gradients[4], gradients[5], gradients[6])
```

```python
import jax
import jax.numpy as jnp
import numpy as np
from jax import lax
from jax.sharding import PartitionSpec as P

epsilon = 1e-06
top_precision = lax.Precision.HIGHEST
f32 = jnp.float32
bf16 = jnp.bfloat16


def bucket_table(length, top_bucket):
    offset = np.arange(length)[:, None] - np.arange(length)[None, :]
    offset = np.maximum(offset, 0)
    octave = offset * 0
    for exponent in range(1, 24):
        octave = octave + (offset >= 2**exponent)
    shifted = offset >> np.maximum(octave - 2, 0)
    logbucket = 16 + 4 * (octave - 4) + (shifted & 3)
    return np.where(offset < 16, offset, np.minimum(logbucket, top_bucket))


def rms_norm(values, gain_vec):
    return (
        values * lax.rsqrt(jnp.mean(values * values, axis=-1, keepdims=True) + epsilon) * gain_vec
    )


def gelu_float(values):
    return jax.nn.gelu(values, approximate=True)


def swap(value, axis, bits):
    size = lax.axis_size(axis)
    return lax.ppermute(value, axis, [(i, i ^ bits) for i in range(size)])


def swap_core(value):
    return swap(value, "dp", 1)


def swap_x(value):
    return swap(value, "dp", 2)


def gather_projections(block):
    experts = lax.axis_size("expert")
    rows, width = block.shape
    if experts != 8:
        full = lax.all_gather(block, ("dp", "expert"), axis=0, tiled=True)
        return full.reshape(4, experts * rows, width)
    far = [swap(block, "expert", bits) for bits in (2, 4, 6)]
    near_y = swap(block, "expert", 1)
    first = jnp.stack([block, near_y])
    first_x = swap_x(first)
    far = jnp.stack(far)
    far_y = swap(far, "expert", 1)
    second = jnp.concatenate([far, far_y])
    second_x = swap_x(second)
    mine = jnp.concatenate([first, second])
    other = jnp.concatenate([first_x, second_x])
    both = jnp.stack([mine, other])
    both_core = swap_core(both)
    pieces = jnp.stack([both, both_core], axis=1).reshape(4, 8, rows, width)
    place = np.array([0, 1, 2, 5, 3, 6, 4, 7])
    dp_order = jnp.arange(4) ^ lax.axis_index("dp")
    expert_order = jnp.asarray(place)[jnp.arange(8) ^ lax.axis_index("expert")]
    flat = (dp_order[:, None] * 8 + expert_order[None, :]).reshape(-1)
    return pieces.reshape(32, rows, width)[flat].reshape(4, 8 * rows, width)


def exchange(chunks):
    experts = lax.axis_size("expert")
    if experts != 8:
        order = jnp.arange(experts) ^ lax.axis_index("expert")
        got = lax.all_to_all(chunks[order], "expert", split_axis=0, concat_axis=0, tiled=True)
        return got[order]
    return jnp.stack([chunks[0]] + [swap(chunks[k], "expert", k) for k in range(1, 8)])


def spread(rows):
    x_rows = swap_x(rows)
    pair = jnp.stack([rows, x_rows])
    core_pair = swap_core(pair)
    return jnp.stack([pair, core_pair], axis=1).reshape((4,) + rows.shape)


def collect(partial):
    parts = partial.reshape((2, 2) + partial.shape[1:])
    from_core = swap_core(parts[:, 1].astype(bf16))
    chip = parts[:, 0] + from_core.astype(f32)
    from_x = swap_x(chip[1].astype(bf16))
    return chip[0] + from_x.astype(f32)


def reduce_experts(grad):
    experts = lax.axis_size("expert")
    rows = grad.shape[0] // experts
    if experts != 8:
        return lax.psum_scatter(grad, "expert", scatter_dimension=0, tiled=True)
    me = lax.axis_index("expert")
    parts = grad.reshape(4, 2, rows, grad.shape[1])
    y_mine = me & 1
    keep = lax.dynamic_index_in_dim(parts, y_mine, 1, keepdims=False)
    send = lax.dynamic_index_in_dim(parts, 1 - y_mine, 1, keepdims=False).astype(bf16)
    pair = keep + swap(send, "expert", 1).astype(f32)
    z_mine = me >> 1
    total = lax.dynamic_index_in_dim(pair, z_mine, 0, keepdims=False)
    for bits in (1, 2, 3):
        part = lax.dynamic_index_in_dim(pair, z_mine ^ bits, 0, keepdims=False).astype(bf16)
        total = total + swap(part, "expert", 2 * bits).astype(f32)
    return total


def sum_all(value):
    for axis in ("dp", "expert"):
        bits = 1
        while bits < lax.axis_size(axis):
            value = value + swap(value, axis, bits)
            bits *= 2
    return value


def shards(
    tokens,
    attn_weights,
    gain_attn,
    gain_ffn,
    rel_table,
    expert_in,
    expert_out,
    gate_weights,
    expert_ids,
    doc_ids,
    cotangent,
):
    seqs, seq_len = doc_ids.shape
    width = tokens.shape[1]
    head_count = rel_table.shape[1]
    head_size = width // head_count
    bucket_count = rel_table.shape[0]
    experts = lax.axis_size("expert")
    token_count = tokens.shape[0]
    block_cap = 3 * seq_len // experts
    capacity = block_cap * seqs
    slots = experts * capacity
    me = lax.axis_index("expert")
    dense = gather_projections(attn_weights)
    w_query, w_key, w_value, w_output = dense[0], dense[1], dense[2], dense[3]
    win, wout = expert_in[0], expert_out[0]

    ids = expert_ids ^ me
    flat_ids = ids.reshape(-1)
    pairs = flat_ids.shape[0]
    earlier = np.tril(np.ones((pairs, pairs), dtype=np.bool_), -1)
    rank = jnp.sum(
        ((flat_ids[:, None] == flat_ids[None, :]) & earlier).astype(jnp.int32), axis=1
    )
    positions = (flat_ids * capacity + rank).reshape(token_count, 2)
    slot_iota = jnp.arange(slots, dtype=jnp.int32)
    first_hit = slot_iota[:, None] == positions[None, :, 0]
    second_hit = slot_iota[:, None] == positions[None, :, 1]
    select = (first_hit | second_hit).astype(bf16)
    gate_slot = jnp.sum(
        jnp.where(first_hit, gate_weights[None, :, 0], 0.0)
        + jnp.where(second_hit, gate_weights[None, :, 1], 0.0),
        axis=1,
    )

    d_buffer = gate_slot[:, None] * jnp.dot(select, cotangent, preferred_element_type=f32)
    d_buffer = d_buffer.astype(bf16).reshape(experts, capacity, width)
    d_buffer, dense = lax.optimization_barrier((d_buffer, dense))
    d_all = spread(exchange(d_buffer)).reshape(-1, width)
    d_hidden = jnp.einsum("rd,fd->rf", d_all, wout, preferred_element_type=f32)

    lookup = np.eye(bucket_count, dtype=np.float32)[
        bucket_table(seq_len, bucket_count - 1).reshape(-1)
    ]
    rel_bias = jnp.dot(
        jnp.asarray(lookup), rel_table, precision=top_precision, preferred_element_type=f32
    )
    rel_bias = rel_bias.reshape(seq_len, seq_len, head_count).transpose(2, 0, 1)
    causal = jnp.asarray(np.tril(np.ones((seq_len, seq_len), dtype=np.int32)) > 0)
    allowed = (doc_ids[:, :, None] == doc_ids[:, None, :]) & causal[None]
    x_float = tokens.astype(f32)
    normed = rms_norm(x_float, gain_attn).astype(bf16)
    shape_heads = (seqs, seq_len, head_count, head_size)

    def heads_of(weights):
        rows = jnp.dot(normed, weights, preferred_element_type=f32)
        return rows.astype(bf16).reshape(shape_heads)

    query_rows, key_rows, value_rows = heads_of(w_query), heads_of(w_key), heads_of(w_value)
    scores = jnp.einsum("sqhd,skhd->shqk", query_rows, key_rows, preferred_element_type=f32)
    scores = jnp.where(allowed[:, None], scores * 0.125 + rel_bias[None], -1000000000.0)
    probs = jax.nn.softmax(scores, axis=-1)
    probs_low = probs.astype(bf16)
    mixed = jnp.einsum("shqk,skhd->sqhd", probs_low, value_rows, preferred_element_type=f32)
    mixed = mixed.astype(bf16).reshape(token_count, width)
    residual = x_float + jnp.dot(mixed, w_output, preferred_element_type=f32)
    moe_in = rms_norm(residual, gain_ffn).astype(bf16)

    buffer = jnp.dot(select, moe_in, preferred_element_type=f32)
    buffer = buffer.astype(bf16).reshape(experts, capacity, width)
    rows = spread(exchange(buffer)).reshape(-1, width)
    pre = jnp.dot(rows, win, preferred_element_type=f32)
    hidden, gelu_back = jax.vjp(gelu_float, pre)
    hidden = hidden.astype(bf16)
    d_pre = gelu_back(d_hidden)[0].astype(bf16)
    d_partial = jnp.einsum("rf,df->rd", d_pre, win, preferred_element_type=f32)
    d_rows = collect(d_partial.reshape(4, experts, capacity, width)).astype(bf16)
    d_returned = exchange(d_rows).reshape(slots, width)
    partial = jnp.dot(hidden, wout, preferred_element_type=f32)
    result = collect(partial.reshape(4, experts, capacity, width)).astype(bf16)
    returned = exchange(result).reshape(slots, width)
    grad_out = jnp.einsum("rf,rd->fd", hidden, d_all, preferred_element_type=f32)
    grad_in = jnp.einsum("rd,rf->df", rows, d_pre, preferred_element_type=f32)

    first_rows = jnp.einsum("st,sd->td", first_hit.astype(bf16), returned, preferred_element_type=f32)
    second_rows = jnp.einsum(
        "st,sd->td", second_hit.astype(bf16), returned, preferred_element_type=f32
    )
    moe_out = gate_weights[:, 0:1] * first_rows + gate_weights[:, 1:2] * second_rows
    output = (residual + moe_out).astype(bf16)

    grad_float = cotangent.astype(f32)
    d_moe_in = jnp.einsum("st,sd->td", select, d_returned, preferred_element_type=f32)
    d_residual_norm, d_gain_ffn = jax.vjp(rms_norm, residual, gain_ffn)[1](d_moe_in)
    d_residual = grad_float + d_residual_norm
    d_attn = d_residual.astype(bf16)
    d_mixed = jnp.einsum("te,de->td", d_attn, w_output, preferred_element_type=f32)
    d_mixed = d_mixed.astype(bf16).reshape(shape_heads)
    d_probs = jnp.einsum("sqhd,skhd->shqk", d_mixed, value_rows, preferred_element_type=f32)
    d_values = jnp.einsum("shqk,sqhd->skhd", probs_low, d_mixed, preferred_element_type=f32)
    d_values = d_values.astype(bf16).reshape(token_count, width)
    d_scores = probs * (d_probs - jnp.sum(probs * d_probs, axis=-1, keepdims=True))
    d_scores = d_scores.astype(bf16)
    d_queries = jnp.einsum("shqk,skhd->sqhd", d_scores, key_rows, preferred_element_type=f32)
    d_queries = (d_queries * 0.125).astype(bf16).reshape(token_count, width)
    d_keys = jnp.einsum("shqk,sqhd->skhd", d_scores, query_rows, preferred_element_type=f32)
    d_keys = (d_keys * 0.125).astype(bf16).reshape(token_count, width)
    d_scores_sum = jnp.sum(d_scores.astype(f32), axis=0)
    d_table = jnp.einsum(
        "hp,pb->bh",
        d_scores_sum.reshape(head_count, seq_len * seq_len),
        lookup,
        precision=top_precision,
        preferred_element_type=f32,
    )
    d_normed = (
        jnp.einsum("te,de->td", d_queries, w_query, preferred_element_type=f32)
        + jnp.einsum("te,de->td", d_keys, w_key, preferred_element_type=f32)
        + jnp.einsum("te,de->td", d_values, w_value, preferred_element_type=f32)
    )
    d_x_norm, d_gain_attn = jax.vjp(rms_norm, x_float, gain_attn)[1](d_normed)
    grad_tokens = d_residual + d_x_norm

    left = spread(jnp.stack([normed, mixed]))
    mine = lax.axis_index("dp")
    left = lax.dynamic_index_in_dim(left, (mine == 3).astype(jnp.int32), 1, keepdims=False)
    grads = jnp.stack([d_queries, d_keys, d_values, d_attn])
    to_x = jnp.where(mine >= 2, grads[0:2], grads[2:4])
    here = jnp.where(mine >= 2, grads[2:4], grads[0:2])
    from_x = swap_x(to_x)
    both = jnp.stack([here, from_x])
    odd = mine & 1
    keep = lax.dynamic_index_in_dim(both, odd, 1, keepdims=False)
    give = lax.dynamic_index_in_dim(both, 1 - odd, 1, keepdims=False)
    got = swap_core(give)
    right = jnp.stack([keep, got], axis=1).reshape(-1, width)
    left = left.reshape(-1, width)
    grad_own = jnp.einsum("td,te->de", left, right, preferred_element_type=f32)
    grad_attn = reduce_experts(grad_own)

    small = jnp.concatenate([d_table.reshape(-1), d_gain_attn, d_gain_ffn])
    small = sum_all(small)
    table_size = bucket_count * head_count
    return (
        output,
        grad_tokens,
        grad_attn,
        small[table_size : table_size + width],
        small[table_size + width :],
        small[0:table_size].reshape(bucket_count, head_count),
        grad_in[None],
        grad_out[None],
    )


def solution(mesh):
    placed = (
        P(("dp", "expert"), None),
        P(("dp", "expert"), None),
        P(),
        P(),
        P(),
        P("expert", None, "dp"),
        P("expert", "dp", None),
        P(("dp", "expert"), None),
        P(("dp", "expert"), None),
        P(("dp", "expert"), None),
        P(("dp", "expert"), None),
    )
    return jax.shard_map(
        shards,
        mesh=mesh,
        in_specs=placed,
        out_specs=(
            P(("dp", "expert"), None),
            P(("dp", "expert"), None),
            P(("dp", "expert"), None),
            P(),
            P(),
            P(),
            P("expert", None, "dp"),
            P("expert", "dp", None),
        ),
        check_vma=False,
    )
```

```python
import jax
import jax.numpy as jnp
import numpy as np
from jax import lax
from jax.experimental import pallas as pl
from jax.experimental.pallas import tpu as pltpu
from jax.sharding import PartitionSpec as P

epsilon = 1e-06
top_precision = lax.Precision.HIGHEST
f32 = jnp.float32
bf16 = jnp.bfloat16


def bucket_table(length, top_bucket):
    offset = np.arange(length)[:, None] - np.arange(length)[None, :]
    offset = np.maximum(offset, 0)
    octave = offset * 0
    for exponent in range(1, 24):
        octave = octave + (offset >= 2**exponent)
    shifted = offset >> np.maximum(octave - 2, 0)
    logbucket = 16 + 4 * (octave - 4) + (shifted & 3)
    return np.where(offset < 16, offset, np.minimum(logbucket, top_bucket))


def swap(value, axis, bits):
    size = lax.axis_size(axis)
    return lax.ppermute(value, axis, [(i, i ^ bits) for i in range(size)])


def swap_core(value):
    return swap(value, "dp", 1)


def swap_x(value):
    return swap(value, "dp", 2)


def gather_projections(block):
    experts = lax.axis_size("expert")
    if experts != 8:
        full = lax.all_gather(block, ("dp", "expert"), axis=0, tiled=True)
        return [full[None]], [None]
    near_y = swap(block, "expert", 1)
    far = jnp.stack([swap(block, "expert", bits) for bits in (2, 4, 6)])
    near = jnp.stack([block, near_y])
    near_x = swap_x(near)
    far, near_x = lax.optimization_barrier((far, near_x))
    far_y = swap(far, "expert", 1)
    far_x = swap_x(far)
    far_yx = swap_x(far_y)
    arrays = [near, near_x, far, far_y, far_x, far_yx]
    offsets = [
        [(0, 0), (0, 1)],
        [(2, 0), (2, 1)],
        [(0, 2), (0, 4), (0, 6)],
        [(0, 3), (0, 5), (0, 7)],
        [(2, 2), (2, 4), (2, 6)],
        [(2, 3), (2, 5), (2, 7)],
    ]
    arrays = arrays + [swap_core(a) for a in arrays]
    offsets = offsets + [[(d + 1, e) for d, e in group] for group in offsets]
    return arrays, offsets


def place_projections(pieces, offsets, dense, sems):
    copies = []
    d_here, e_here = lax.axis_index("dp"), lax.axis_index("expert")
    experts = lax.axis_size("expert")
    for piece, group in zip(pieces, offsets):
        rows = piece.shape[1]
        for i in range(piece.shape[0]):
            target = dense
            if group is not None:
                block = (d_here ^ group[i][0]) * experts + (e_here ^ group[i][1])
                target = dense.at[pl.ds(pl.multiple_of(block * rows, rows), rows)]
            copies.append(pltpu.make_async_copy(piece.at[i], target, sems.at[len(copies)]))
    for copy in copies:
        copy.start()
    return copies


VMEM = pl.BlockSpec(memory_space=pltpu.VMEM)
ANY = pl.BlockSpec(memory_space=pl.ANY)
LIMIT = pltpu.CompilerParams(vmem_limit_bytes=58 * 1024 * 1024)


def dot(a, b):
    return jnp.dot(a, b, preferred_element_type=f32)


def dot_t(a, b):
    return lax.dot_general(a, b, (((1,), (1,)), ((), ())), preferred_element_type=f32)


def t_dot(a, b):
    return lax.dot_general(a, b, (((0,), (0,)), ((), ())), preferred_element_type=f32)


def inverse_rms(values):
    return lax.rsqrt(jnp.mean(values * values, axis=-1, keepdims=True) + epsilon)


def attention_forward(pieces, offsets, tokens, gains, bias_rows, docs_col, docs_row, select, heads):
    count, width = tokens.shape
    slots = select.shape[0]
    blocks = sum(p.shape[0] for p in pieces)
    n = len(pieces)

    def kernel(*refs):
        piece_refs, refs = refs[:n], refs[n:]
        tok, gain, bias, dcol, drow, sel = refs[:6]
        normed_o, qkv_o, mixed_o, probs_o, residual_o, buffer_o, dense, sems = refs[6:]
        copies = place_projections(piece_refs, offsets, dense, sems)
        x = tok[...].astype(f32)
        normed = (x * inverse_rms(x) * gain[0:1, :]).astype(bf16)
        normed_o[...] = normed
        row = lax.broadcasted_iota(jnp.int32, (count, count), 0)
        col = lax.broadcasted_iota(jnp.int32, (count, count), 1)
        allowed = (dcol[...] == drow[...]) & (col <= row)
        low_lanes = lax.broadcasted_iota(jnp.int32, (count, 128), 1) < 64
        for copy in copies:
            copy.wait()
        for i in range(3):
            qkv_o[i] = dot(normed, dense[i * width : (i + 1) * width, :]).astype(bf16)
        for pair in range(heads // 2):
            lanes = slice(128 * pair, 128 * pair + 128)
            q, k, v = qkv_o[0, :, lanes], qkv_o[1, :, lanes], qkv_o[2, :, lanes]
            out = []
            for half in range(2):
                mask = low_lanes if half == 0 else ~low_lanes
                head = 2 * pair + half
                shift = jnp.broadcast_to(bias[head : head + 1, :], (count, 128))
                shift = pltpu.roll(shift, 0, 1, stride=1, stride_axis=0)
                scores = dot_t(jnp.where(mask, q, jnp.zeros_like(q)), k) * 0.125 + shift
                scores = jnp.where(allowed, scores, -1000000000.0)
                scores = jnp.exp(scores - jnp.max(scores, axis=-1, keepdims=True))
                probs = scores / jnp.sum(scores, axis=-1, keepdims=True)
                probs_o[head] = probs
                out.append(dot(probs.astype(bf16), v))
            mixed_o[:, lanes] = jnp.where(low_lanes, out[0], out[1]).astype(bf16)
        residual = x + dot(mixed_o[...], dense[3 * width : 4 * width, :])
        residual_o[...] = residual
        moe_in = (residual * inverse_rms(residual) * gain[1:2, :]).astype(bf16)
        buffer_o[...] = dot(sel[...], moe_in).astype(bf16)

    return pl.pallas_call(
        kernel,
        out_shape=(
            jax.ShapeDtypeStruct((count, width), bf16),
            jax.ShapeDtypeStruct((3, count, width), bf16),
            jax.ShapeDtypeStruct((count, width), bf16),
            jax.ShapeDtypeStruct((heads, count, count), f32),
            jax.ShapeDtypeStruct((count, width), f32),
            jax.ShapeDtypeStruct((slots, width), bf16),
        ),
        in_specs=[ANY] * n + [VMEM] * 6,
        out_specs=(VMEM,) * 6,
        scratch_shapes=[
            pltpu.VMEM((4 * width, width), bf16),
            pltpu.SemaphoreType.DMA((blocks,)),
        ],
        compiler_params=LIMIT,
        name="attention_forward",
    )(*pieces, tokens, gains, bias_rows, docs_col, docs_row, select)


def attention_backward(
    pieces, offsets, tokens, gains, cotangent, residual, d_returned, select_t, qkv, probs, heads
):
    count, width = tokens.shape
    blocks = sum(p.shape[0] for p in pieces)
    n = len(pieces)

    def kernel(*refs):
        piece_refs, refs = refs[:n], refs[n:]
        tok, gain, cot, res, d_ret, sel_t, qkv_r, probs_r = refs[:8]
        grads_o, d_tok_o, diag_o, d_gain_o, dense, d_mixed_s, sems = refs[8:]
        copies = place_projections(piece_refs, offsets, dense, sems)
        d_moe = dot(sel_t[...], d_ret[...])
        residual = res[...]
        r = inverse_rms(residual)
        d_gain_o[1:2, :] = jnp.sum(d_moe * residual * r, axis=0, keepdims=True)
        m = d_moe * gain[1:2, :]
        mean = jnp.mean(m * residual, axis=-1, keepdims=True)
        d_residual = cot[...].astype(f32) + r * m - r * r * r * residual * mean
        d_tok_o[...] = d_residual
        d_attn = d_residual.astype(bf16)
        grads_o[3] = d_attn
        for copy in copies:
            copy.wait()
        d_mixed_s[...] = dot_t(d_attn, dense[3 * width : 4 * width, :]).astype(bf16)
        low_lanes = lax.broadcasted_iota(jnp.int32, (count, 128), 1) < 64
        row = lax.broadcasted_iota(jnp.int32, (count, count), 0)
        for pair in range(heads // 2):
            lanes = slice(128 * pair, 128 * pair + 128)
            q, k, v = qkv_r[0, :, lanes], qkv_r[1, :, lanes], qkv_r[2, :, lanes]
            d_mix = d_mixed_s[:, lanes]
            d_q, d_k, d_v = [], [], []
            for half in range(2):
                mask = low_lanes if half == 0 else ~low_lanes
                head = 2 * pair + half
                probs = probs_r[head]
                d_probs = dot_t(jnp.where(mask, d_mix, jnp.zeros_like(d_mix)), v)
                d_v.append(t_dot(probs.astype(bf16), d_mix))
                inner = jnp.sum(probs * d_probs, axis=-1, keepdims=True)
                d_scores = (probs * (d_probs - inner)).astype(bf16)
                d_q.append(dot(d_scores, k))
                d_k.append(t_dot(d_scores, q))
                turned = d_scores.astype(f32)
                for bit in (1, 2, 4, 8, 16, 32, 64):
                    turned = jnp.where(
                        (row & bit) != 0, pltpu.roll(turned, count - bit, 1), turned
                    )
                diag_o[head : head + 1, :] = jnp.sum(turned, axis=0, keepdims=True)
            grads_o[0, :, lanes] = (jnp.where(low_lanes, d_q[0], d_q[1]) * 0.125).astype(bf16)
            grads_o[1, :, lanes] = (jnp.where(low_lanes, d_k[0], d_k[1]) * 0.125).astype(bf16)
            grads_o[2, :, lanes] = jnp.where(low_lanes, d_v[0], d_v[1]).astype(bf16)
        d_normed = dot_t(grads_o[0], dense[0:width, :])
        d_normed = d_normed + dot_t(grads_o[1], dense[width : 2 * width, :])
        d_normed = d_normed + dot_t(grads_o[2], dense[2 * width : 3 * width, :])
        x = tok[...].astype(f32)
        s = inverse_rms(x)
        d_gain_o[0:1, :] = jnp.sum(d_normed * x * s, axis=0, keepdims=True)
        m = d_normed * gain[0:1, :]
        mean = jnp.mean(m * x, axis=-1, keepdims=True)
        d_tok_o[...] += s * m - s * s * s * x * mean

    return pl.pallas_call(
        kernel,
        out_shape=(
            jax.ShapeDtypeStruct((4, count, width), bf16),
            jax.ShapeDtypeStruct((count, width), f32),
            jax.ShapeDtypeStruct((heads, count), f32),
            jax.ShapeDtypeStruct((2, width), f32),
        ),
        in_specs=[ANY] * n + [VMEM] * 8,
        out_specs=(VMEM,) * 4,
        scratch_shapes=[
            pltpu.VMEM((4 * width, width), bf16),
            pltpu.VMEM((count, width), bf16),
            pltpu.SemaphoreType.DMA((blocks,)),
        ],
        compiler_params=LIMIT,
        name="attention_backward",
    )(*pieces, tokens, gains, cotangent, residual, d_returned, select_t, qkv, probs)


def gelu_parts(v):
    c = 0.7978845608028654
    square = v * v
    t = jnp.tanh(c * v * (1.0 + 0.044715 * square))
    half = 0.5 * (1.0 + t)
    slope = half + 0.5 * v * (1.0 - t * t) * (c + (3.0 * 0.044715 * c) * square)
    return v * half, slope


def experts_first(rows, d_rows, win, wout):
    count, width = rows[0].shape
    units = win.shape[1]

    def kernel(*refs):
        row_refs, d_refs, (win_r, wout_r) = refs[0:4], refs[4:8], refs[8:10]
        hidden_o, d_pre_o, keep_o, send_o, row_s, d_s, win_s, wout_s, sems = refs[10:]
        copies = [
            pltpu.make_async_copy(win_r, win_s, sems.at[8]),
            pltpu.make_async_copy(wout_r, wout_s, sems.at[9]),
        ]
        order = (1, 3, 0, 2)
        for i in order:
            copies.append(pltpu.make_async_copy(row_refs[i], row_s.at[i], sems.at[i]))
            copies.append(pltpu.make_async_copy(d_refs[i], d_s.at[i], sems.at[4 + i]))
        for copy in copies:
            copy.start()
        copies[0].wait()
        copies[1].wait()
        for n, i in enumerate(order):
            copies[2 + 2 * n].wait()
            copies[3 + 2 * n].wait()
            pre = dot(row_s[i], win_s[...])
            d_hidden = dot_t(d_s[i], wout_s[...])
            hidden, slope = gelu_parts(pre)
            hidden_o[i] = hidden.astype(bf16)
            d_pre = (d_hidden * slope).astype(bf16)
            d_pre_o[i] = d_pre
            d_slot = dot_t(d_pre, win_s[...])
            if i % 2 == 1:
                send_o[i // 2] = d_slot.astype(bf16)
            else:
                keep_o[i // 2] = d_slot

    return pl.pallas_call(
        kernel,
        out_shape=(
            jax.ShapeDtypeStruct((4, count, units), bf16),
            jax.ShapeDtypeStruct((4, count, units), bf16),
            jax.ShapeDtypeStruct((2, count, width), f32),
            jax.ShapeDtypeStruct((2, count, width), bf16),
        ),
        in_specs=[ANY] * 10,
        out_specs=(VMEM,) * 4,
        scratch_shapes=[
            pltpu.VMEM((4, count, width), bf16),
            pltpu.VMEM((4, count, width), bf16),
            pltpu.VMEM(win.shape, bf16),
            pltpu.VMEM(wout.shape, bf16),
            pltpu.SemaphoreType.DMA((10,)),
        ],
        compiler_params=LIMIT,
        name="experts_first",
    )(*rows, *d_rows, win, wout)


def experts_second(rows, d_rows, hidden, d_pre, wout):
    count, width = rows[0].shape
    units = wout.shape[0]

    def kernel(*refs):
        row_refs, d_refs, (hidden_r, d_pre_r, wout_r) = refs[0:4], refs[4:8], refs[8:11]
        keep_o, send_o, in_o, out_o = refs[11:]
        for i in (1, 3, 0, 2):
            result = dot(hidden_r[i], wout_r[...])
            if i % 2 == 1:
                send_o[i // 2] = result.astype(bf16)
            else:
                keep_o[i // 2] = result
        for i in range(4):
            g_in = t_dot(row_refs[i][...], d_pre_r[i])
            g_out = t_dot(hidden_r[i], d_refs[i][...])
            if i == 0:
                in_o[...] = g_in
                out_o[...] = g_out
            else:
                in_o[...] += g_in
                out_o[...] += g_out

    return pl.pallas_call(
        kernel,
        out_shape=(
            jax.ShapeDtypeStruct((2, count, width), f32),
            jax.ShapeDtypeStruct((2, count, width), bf16),
            jax.ShapeDtypeStruct((width, units), f32),
            jax.ShapeDtypeStruct((units, width), f32),
        ),
        in_specs=[VMEM] * 11,
        out_specs=(VMEM,) * 4,
        compiler_params=LIMIT,
        name="experts_second",
    )(*rows, *d_rows, hidden, d_pre, wout)


def exchange_plain(chunks):
    return lax.all_to_all(chunks, "expert", split_axis=0, concat_axis=0, tiled=True)


def exchange_apart(chunks):
    experts = lax.axis_size("expert")
    if experts != 8:
        return exchange_plain(chunks)
    me = lax.axis_index("expert")
    out = jnp.zeros_like(chunks)
    own = lax.dynamic_index_in_dim(chunks, me, 0, keepdims=True)
    out = lax.dynamic_update_slice_in_dim(out, own, me, 0)
    for bits in (6, 4, 7, 5, 2, 3, 1):
        part = lax.dynamic_index_in_dim(chunks, me ^ bits, 0, keepdims=True)
        out = lax.dynamic_update_slice_in_dim(out, swap(part, "expert", bits), me ^ bits, 0)
    return out


def spread(rows):
    x_rows = swap_x(rows)
    return [rows, swap_core(rows), x_rows, swap_core(x_rows)]


def collect(keep, send):
    from_core = swap_core(send)
    chip_x = (keep[1] + from_core[1].astype(f32)).astype(bf16)
    from_x = swap_x(chip_x)
    return (keep[0] + from_core[0].astype(f32) + from_x.astype(f32)).astype(bf16)


def reduce_experts(grad):
    experts = lax.axis_size("expert")
    rows = grad.shape[0] // experts
    if experts != 8:
        return lax.psum_scatter(grad, "expert", scatter_dimension=0, tiled=True)
    me = lax.axis_index("expert")
    parts = grad.reshape(4, 2, rows, grad.shape[1])
    y_mine = me & 1
    keep = lax.dynamic_index_in_dim(parts, y_mine, 1, keepdims=False)
    send = lax.dynamic_index_in_dim(parts, 1 - y_mine, 1, keepdims=False).astype(bf16)
    pair = keep + swap(send, "expert", 1).astype(f32)
    z_mine = me >> 1
    total = lax.dynamic_index_in_dim(pair, z_mine, 0, keepdims=False)
    for bits in (1, 2, 3):
        part = lax.dynamic_index_in_dim(pair, z_mine ^ bits, 0, keepdims=False).astype(bf16)
        total = total + swap(part, "expert", 2 * bits).astype(f32)
    return total


def sum_all(value):
    for axis in ("dp", "expert"):
        bits = 1
        while bits < lax.axis_size(axis):
            value = value + swap(value, axis, bits)
            bits *= 2
    return value


def shards(
    tokens,
    attn_weights,
    gain_attn,
    gain_ffn,
    rel_table,
    expert_in,
    expert_out,
    gate_weights,
    expert_ids,
    doc_ids,
    cotangent,
):
    seqs, seq_len = doc_ids.shape
    width = tokens.shape[1]
    head_count = rel_table.shape[1]
    head_size = width // head_count
    bucket_count = rel_table.shape[0]
    experts = lax.axis_size("expert")
    token_count = tokens.shape[0]
    block_cap = 3 * seq_len // experts
    capacity = block_cap * seqs
    slots = experts * capacity
    pieces, offsets = gather_projections(attn_weights)
    win, wout = expert_in[0], expert_out[0]

    flat_ids = expert_ids.reshape(-1)
    pairs = flat_ids.shape[0]
    earlier = np.tril(np.ones((pairs, pairs), dtype=np.bool_), -1)
    rank = jnp.sum(
        ((flat_ids[:, None] == flat_ids[None, :]) & earlier).astype(jnp.int32), axis=1
    )
    positions = (flat_ids * capacity + rank).reshape(token_count, 2)
    slot_iota = jnp.arange(slots, dtype=jnp.int32)
    first_hit = slot_iota[:, None] == positions[None, :, 0]
    second_hit = slot_iota[:, None] == positions[None, :, 1]
    select = (first_hit | second_hit).astype(bf16)
    first_t = (slot_iota[None, :] == positions[:, 0:1]).astype(bf16)
    second_t = (slot_iota[None, :] == positions[:, 1:2]).astype(bf16)
    select_t = first_t + second_t
    gate_slot = jnp.sum(
        jnp.where(first_hit, gate_weights[None, :, 0], 0.0)
        + jnp.where(second_hit, gate_weights[None, :, 1], 0.0),
        axis=1,
    )

    def to_experts(buffer):
        got = exchange_plain(buffer.reshape(experts, capacity, width))
        return spread(got.reshape(slots, width))

    def to_tokens(rows, move):
        return move(rows.reshape(experts, capacity, width)).reshape(slots, width)

    d_buffer = gate_slot[:, None] * jnp.dot(select, cotangent, preferred_element_type=f32)
    d_buffer = d_buffer.astype(bf16)
    d_buffer, pieces = lax.optimization_barrier((d_buffer, pieces))
    d_all = to_experts(d_buffer)

    distance = (token_count - np.arange(token_count)) % token_count
    lookup = np.eye(bucket_count, dtype=np.float32)[
        bucket_table(seq_len, bucket_count - 1)[np.minimum(distance, seq_len - 1), 0]
    ]
    lookup = jnp.asarray(lookup * (distance < seq_len)[:, None])
    bias_rows = lax.dot_general(
        rel_table,
        lookup,
        (((0,), (1,)), ((), ())),
        precision=top_precision,
        preferred_element_type=f32,
    )
    gains = jnp.stack([gain_attn, gain_ffn])
    docs = doc_ids + 4 * jnp.arange(seqs, dtype=jnp.int32)[:, None]
    docs_col, docs_row = docs.reshape(-1, 1), docs.reshape(1, -1)
    normed, qkv, mixed, probs, residual, buffer = attention_forward(
        pieces, offsets, tokens, gains, bias_rows, docs_col, docs_row, select, head_count
    )

    rows = to_experts(buffer)
    hidden, d_pre, keep, send = experts_first(rows, d_all, win, wout)
    d_returned = to_tokens(collect(keep, send), exchange_plain)
    keep, send, grad_in, grad_out = experts_second(rows, d_all, hidden, d_pre, wout)
    result = collect(keep, send)
    result, d_returned = lax.optimization_barrier((result, d_returned))
    returned = to_tokens(result, exchange_apart)
    moe_out = gate_weights[:, 0:1] * jnp.dot(first_t, returned, preferred_element_type=f32)
    moe_out = moe_out + gate_weights[:, 1:2] * jnp.dot(
        second_t, returned, preferred_element_type=f32
    )
    output = (residual + moe_out).astype(bf16)

    grads, grad_tokens, diagonals, d_gains = attention_backward(
        pieces,
        offsets,
        tokens,
        gains,
        cotangent,
        residual,
        d_returned,
        select_t,
        qkv,
        probs,
        head_count,
    )

    mine = lax.axis_index("dp")
    left = jnp.stack([normed, mixed])
    left_x = swap_x(left)
    left = jnp.stack([left, left_x], axis=1)
    left_core = swap_core(left)
    left = jnp.where(mine == 3, jnp.stack([left[1], left_core[1]]), jnp.stack([left[0], left_core[0]]))
    to_x = jnp.where(mine >= 2, grads[0:2], grads[2:4])
    here = jnp.where(mine >= 2, grads[2:4], grads[0:2])
    from_x = swap_x(to_x)
    odd = (mine & 1) == 1
    keep = jnp.stack([jnp.where(odd, here[1], here[0]), jnp.where(odd, from_x[1], from_x[0])])
    give = jnp.stack([jnp.where(odd, here[0], here[1]), jnp.where(odd, from_x[0], from_x[1])])
    got = swap_core(give)
    right = jnp.stack([keep, got]).reshape(-1, width)
    left = left.reshape(-1, width)
    grad_own = jnp.einsum("td,te->de", left, right, preferred_element_type=f32)
    grad_attn = reduce_experts(grad_own)

    small = jnp.concatenate([diagonals.reshape(-1), d_gains.reshape(-1)])
    small = sum_all(small)
    diagonals = small[0 : head_count * token_count].reshape(head_count, token_count)
    d_gains = small[head_count * token_count :].reshape(2, width)
    d_table = lax.dot_general(
        lookup,
        diagonals,
        (((0,), (1,)), ((), ())),
        precision=top_precision,
        preferred_element_type=f32,
    )
    return (
        output,
        grad_tokens,
        grad_attn,
        d_gains[0],
        d_gains[1],
        d_table,
        grad_in[None],
        grad_out[None],
    )


def solution(mesh):
    placed = (
        P(("dp", "expert"), None),
        P(("dp", "expert"), None),
        P(),
        P(),
        P(),
        P("expert", None, "dp"),
        P("expert", "dp", None),
        P(("dp", "expert"), None),
        P(("dp", "expert"), None),
        P(("dp", "expert"), None),
        P(("dp", "expert"), None),
    )
    return jax.shard_map(
        shards,
        mesh=mesh,
        in_specs=placed,
        out_specs=(
            P(("dp", "expert"), None),
            P(("dp", "expert"), None),
            P(("dp", "expert"), None),
            P(),
            P(),
            P(),
            P("expert", None, "dp"),
            P("expert", "dp", None),
        ),
        check_vma=False,
    )
```

```python
import jax
import jax.numpy as jnp
import numpy as np
from jax import lax
from jax.experimental import pallas as pl
from jax.experimental.pallas import tpu as pltpu
from jax.sharding import PartitionSpec as P

epsilon = 1e-06
top_precision = lax.Precision.HIGHEST
f32 = jnp.float32
bf16 = jnp.bfloat16


def bucket_table(length, top_bucket):
    offset = np.arange(length)[:, None] - np.arange(length)[None, :]
    offset = np.maximum(offset, 0)
    octave = offset * 0
    for exponent in range(1, 24):
        octave = octave + (offset >= 2**exponent)
    shifted = offset >> np.maximum(octave - 2, 0)
    logbucket = 16 + 4 * (octave - 4) + (shifted & 3)
    return np.where(offset < 16, offset, np.minimum(logbucket, top_bucket))


def swap(value, axis, bits):
    size = lax.axis_size(axis)
    return lax.ppermute(value, axis, [(i, i ^ bits) for i in range(size)])


def swap_core(value):
    return swap(value, "dp", 1)


def swap_x(value):
    return swap(value, "dp", 2)


def gather_projections(block, d_buffer, prepared):
    experts = lax.axis_size("expert")
    if experts != 8:
        full = lax.all_gather(block, ("dp", "expert"), axis=0, tiled=True)
        return [full[None]], [None], exchange_plain(d_buffer), prepared
    first = [swap(block, "expert", bits) for bits in (4, 6, 2, 1)] + [swap_x(block)]
    first, prepared = lax.optimization_barrier((first, prepared))
    z_far, z_last, z_near, near_y, near_x = first
    two = jnp.stack([z_far, z_near])
    two_y = swap(two, "expert", 1)
    two_x = swap_x(two)
    last_x = swap_x(z_last)
    last_y = swap(z_last, "expert", 1)
    near_xy = swap(near_x, "expert", 1)
    two_y, last_x = lax.optimization_barrier((two_y, last_x))
    two_yx = swap_x(two_y)
    last_xy = swap(last_x, "expert", 1)
    two_x, d_buffer = lax.optimization_barrier((two_x, d_buffer))
    d_got = exchange_plain(d_buffer)
    one = jnp.stack([block, near_y, near_x])
    arrays = [one, two, two_y, two_x, two_yx]
    offsets = [
        [(0, 0), (0, 1), (2, 0)],
        [(0, 4), (0, 2)],
        [(0, 5), (0, 3)],
        [(2, 4), (2, 2)],
        [(2, 5), (2, 3)],
    ]
    rest = jnp.stack([z_last, last_x, last_y, near_xy])
    arrays = arrays + [rest, last_xy[None]]
    offsets = offsets + [[(0, 6), (2, 6), (0, 7), (2, 1)], [(2, 7)]]
    arrays = arrays + [swap_core(a) for a in arrays]
    offsets = offsets + [[(d + 1, e) for d, e in group] for group in offsets]
    return arrays, offsets, d_got, prepared


def place_projections(pieces, offsets, dense, sems):
    copies = []
    d_here, e_here = lax.axis_index("dp"), lax.axis_index("expert")
    experts = lax.axis_size("expert")
    for piece, group in zip(pieces, offsets):
        rows = piece.shape[1]
        for i in range(piece.shape[0]):
            target = dense
            if group is not None:
                block = (d_here ^ group[i][0]) * experts + (e_here ^ group[i][1])
                target = dense.at[pl.ds(pl.multiple_of(block * rows, rows), rows)]
            copies.append(pltpu.make_async_copy(piece.at[i], target, sems.at[len(copies)]))
    for copy in copies:
        copy.start()
    return copies


VMEM = pl.BlockSpec(memory_space=pltpu.VMEM)
ANY = pl.BlockSpec(memory_space=pl.ANY)
LIMIT = pltpu.CompilerParams(vmem_limit_bytes=58 * 1024 * 1024)


def cost(microseconds):
    return pl.CostEstimate(
        flops=int(microseconds * 1.0e9), bytes_accessed=int(microseconds * 3.0e6), transcendentals=0
    )


def dot(a, b):
    return jnp.dot(a, b, preferred_element_type=f32)


def dot_t(a, b):
    return lax.dot_general(a, b, (((1,), (1,)), ((), ())), preferred_element_type=f32)


def t_dot(a, b):
    return lax.dot_general(a, b, (((0,), (0,)), ((), ())), preferred_element_type=f32)


def inverse_rms(values):
    return lax.rsqrt(jnp.mean(values * values, axis=-1, keepdims=True) + epsilon)


def attention_forward(
    pieces, offsets, tokens, gains, bias_rows, docs_row, select, heads
):
    count, width = tokens.shape
    slots = select.shape[0]
    blocks = sum(p.shape[0] for p in pieces)
    n = len(pieces)

    def kernel(*refs):
        piece_refs, refs = refs[:n], refs[n:]
        tok, gain, bias, drow, sel = refs[:5]
        normed_o, mixed_o, qkv_o, probs_o, residual_o, buffer_o, dense, sems = refs[5:]
        copies = place_projections(piece_refs, offsets, dense, sems)
        x = tok[...].astype(f32)
        normed = (x * inverse_rms(x) * gain[0:1, :]).astype(bf16)
        normed_o[...] = normed
        row = lax.broadcasted_iota(jnp.int32, (count, count), 0)
        col = lax.broadcasted_iota(jnp.int32, (count, count), 1)
        docs = jnp.broadcast_to(drow[...], (count, count))
        allowed = (docs == docs.T) & (col <= row)
        low_lanes = lax.broadcasted_iota(jnp.int32, (count, 128), 1) < 64
        for copy in copies:
            copy.wait()
        for i in range(3):
            qkv_o[i] = dot(normed, dense[i * width : (i + 1) * width, :]).astype(bf16)
        for pair in range(heads // 2):
            lanes = slice(128 * pair, 128 * pair + 128)
            q, k, v = qkv_o[0, :, lanes], qkv_o[1, :, lanes], qkv_o[2, :, lanes]
            out = []
            for half in range(2):
                mask = low_lanes if half == 0 else ~low_lanes
                head = 2 * pair + half
                shift = jnp.broadcast_to(bias[head : head + 1, :], (count, 128))
                shift = pltpu.roll(shift, 0, 1, stride=1, stride_axis=0)
                scores = dot_t(jnp.where(mask, q, jnp.zeros_like(q)), k) * 0.125 + shift
                scores = jnp.where(allowed, scores, -1000000000.0)
                scores = jnp.exp(scores - jnp.max(scores, axis=-1, keepdims=True))
                probs = scores / jnp.sum(scores, axis=-1, keepdims=True)
                probs_o[head] = probs
                out.append(dot(probs.astype(bf16), v))
            mixed_o[:, lanes] = jnp.where(low_lanes, out[0], out[1]).astype(bf16)
        residual = x + dot(mixed_o[...], dense[3 * width : 4 * width, :])
        residual_o[...] = residual
        moe_in = (residual * inverse_rms(residual) * gain[1:2, :]).astype(bf16)
        buffer_o[...] = dot(sel[...], moe_in).astype(bf16)

    return pl.pallas_call(
        kernel,
        out_shape=(
            jax.ShapeDtypeStruct((count, width), bf16),
            jax.ShapeDtypeStruct((count, width), bf16),
            jax.ShapeDtypeStruct((3, count, width), bf16),
            jax.ShapeDtypeStruct((heads, count, count), f32),
            jax.ShapeDtypeStruct((count, width), f32),
            jax.ShapeDtypeStruct((slots, width), bf16),
        ),
        in_specs=[ANY] * n + [VMEM] * 5,
        out_specs=(VMEM,) * 6,
        scratch_shapes=[
            pltpu.VMEM((4 * width, width), bf16),
            pltpu.SemaphoreType.DMA((blocks,)),
        ],
        compiler_params=LIMIT,
        cost_estimate=cost(3),
        name="attention_forward",
    )(*pieces, tokens, gains, bias_rows, docs_row, select)


def attention_backward(
    pieces, offsets, tokens, gains, cotangent, residual, d_returned, select_t, qkv, probs, heads
):
    count, width = tokens.shape
    blocks = sum(p.shape[0] for p in pieces)
    n = len(pieces)

    def kernel(*refs):
        piece_refs, refs = refs[:n], refs[n:]
        tok, gain, cot, res, d_ret, sel_t, qkv_r, probs_r = refs[:8]
        outs, (d_tok_o, small_o) = refs[8:12], refs[12:14]
        dense, d_mixed_s, grads_o, packed_s, sems = refs[14:]
        d_here = lax.axis_index("dp")
        copies = place_projections(piece_refs, offsets, dense, sems)
        d_moe = dot(sel_t[...], d_ret[...])
        residual = res[...]
        r = inverse_rms(residual)
        small_o[3:4, :] = jnp.sum(d_moe * residual * r, axis=0, keepdims=True)
        m = d_moe * gain[1:2, :]
        mean = jnp.mean(m * residual, axis=-1, keepdims=True)
        d_residual = cot[...].astype(f32) + r * m - r * r * r * residual * mean
        d_tok_o[...] = d_residual
        d_attn = d_residual.astype(bf16)
        grads_o[d_here ^ 3] = d_attn
        for copy in copies:
            copy.wait()
        d_mixed_s[...] = dot_t(d_attn, dense[3 * width : 4 * width, :]).astype(bf16)
        low_lanes = lax.broadcasted_iota(jnp.int32, (count, 128), 1) < 64
        row = lax.broadcasted_iota(jnp.int32, (count, count), 0)
        for pair in range(heads // 2):
            lanes = slice(128 * pair, 128 * pair + 128)
            q, k, v = qkv_r[0, :, lanes], qkv_r[1, :, lanes], qkv_r[2, :, lanes]
            d_mix = d_mixed_s[:, lanes]
            d_q, d_k, d_v = [], [], []
            for half in range(2):
                mask = low_lanes if half == 0 else ~low_lanes
                head = 2 * pair + half
                probs = probs_r[head]
                d_probs = dot_t(jnp.where(mask, d_mix, jnp.zeros_like(d_mix)), v)
                d_v.append(t_dot(probs.astype(bf16), d_mix))
                inner = jnp.sum(probs * d_probs, axis=-1, keepdims=True)
                d_scores = (probs * (d_probs - inner)).astype(bf16)
                d_q.append(dot(d_scores, k))
                d_k.append(t_dot(d_scores, q))
                turned = d_scores.astype(f32)
                for bit in (1, 2, 4, 8, 16, 32, 64):
                    turned = jnp.where(
                        (row & bit) != 0, pltpu.roll(turned, count - bit, 1), turned
                    )
                at, slot = head // 6, 128 * (head % 6)
                small_o[at : at + 1, slot : slot + 128] = jnp.sum(turned, axis=0, keepdims=True)
            grads_o[d_here ^ 0, :, lanes] = (jnp.where(low_lanes, d_q[0], d_q[1]) * 0.125).astype(bf16)
            grads_o[d_here ^ 1, :, lanes] = (jnp.where(low_lanes, d_k[0], d_k[1]) * 0.125).astype(bf16)
            grads_o[d_here ^ 2, :, lanes] = jnp.where(low_lanes, d_v[0], d_v[1]).astype(bf16)
        outs[0][...] = grads_o[0]
        d_normed = dot_t(grads_o[d_here ^ 0], dense[0:width, :])
        d_normed = d_normed + dot_t(grads_o[d_here ^ 1], dense[width : 2 * width, :])
        d_normed = d_normed + dot_t(grads_o[d_here ^ 2], dense[2 * width : 3 * width, :])
        x = tok[...].astype(f32)
        s = inverse_rms(x)
        small_o[2:3, :] = jnp.sum(d_normed * x * s, axis=0, keepdims=True)
        m = d_normed * gain[0:1, :]
        mean = jnp.mean(m * x, axis=-1, keepdims=True)
        d_tok_o[...] += s * m - s * s * s * x * mean
        small = small_o[0:4, :]
        high = small.astype(bf16).astype(f32)
        packed_s[...] = jnp.zeros_like(packed_s)
        packed_s[0:4, :] = high
        packed_s[4:8, :] = small - high
        for i in range(1, 4):
            outs[i][0:count, :] = grads_o[i]
            outs[i][count:, :] = packed_s[...].astype(bf16)

    return pl.pallas_call(
        kernel,
        out_shape=(jax.ShapeDtypeStruct((count, width), bf16),)
        + (jax.ShapeDtypeStruct((count + 16, width), bf16),) * 3
        + (
            jax.ShapeDtypeStruct((count, width), f32),
            jax.ShapeDtypeStruct((8, width), f32),
        ),
        in_specs=[ANY] * n + [VMEM] * 8,
        out_specs=(VMEM,) * 6,
        scratch_shapes=[
            pltpu.VMEM((4 * width, width), bf16),
            pltpu.VMEM((count, width), bf16),
            pltpu.VMEM((4, count, width), bf16),
            pltpu.VMEM((16, width), f32),
            pltpu.SemaphoreType.DMA((blocks,)),
        ],
        compiler_params=LIMIT,
        cost_estimate=cost(13),
        name="attention_backward",
    )(*pieces, tokens, gains, cotangent, residual, d_returned, select_t, qkv, probs)


def gelu_parts(v):
    c = 0.7978845608028654
    square = v * v
    t = jnp.tanh(c * v * (1.0 + 0.044715 * square))
    half = 0.5 * (1.0 + t)
    slope = half + 0.5 * v * (1.0 - t * t) * (c + (3.0 * 0.044715 * c) * square)
    return v * half, slope


def experts_first(rows, d_rows, win, wout):
    count, width = rows[0].shape
    units = win.shape[1]

    def kernel(*refs):
        row_refs, d_refs, (win_r, wout_r) = refs[0:2], refs[2:4], refs[4:6]
        hidden_o, d_pre_o, keep_o, send_o, row_s, d_s, win_s, wout_s, sems = refs[6:]
        sources = (d_refs[1], wout_r, row_refs[1], win_r, d_refs[0], row_refs[0])
        targets = (d_s.at[1], wout_s, row_s.at[1], win_s, d_s.at[0], row_s.at[0])
        copies = [
            pltpu.make_async_copy(source, target, sems.at[n])
            for n, (source, target) in enumerate(zip(sources, targets))
        ]
        for copy in copies:
            copy.start()
        for i in (1, 0):
            for copy in copies[0:4] if i else copies[4:6]:
                copy.wait()
            d_hidden = dot_t(d_s[i], wout_s[...])
            pre = dot(row_s[i], win_s[...])
            hidden, slope = gelu_parts(pre)
            hidden_o[i] = hidden.astype(bf16)
            d_pre = (d_hidden * slope).astype(bf16)
            d_pre_o[i] = d_pre
            d_slot = dot_t(d_pre, win_s[...])
            if i == 1:
                send_o[...] = d_slot.astype(bf16)
            else:
                keep_o[...] = d_slot

    return pl.pallas_call(
        kernel,
        out_shape=(
            jax.ShapeDtypeStruct((2, count, units), bf16),
            jax.ShapeDtypeStruct((2, count, units), bf16),
            jax.ShapeDtypeStruct((count, width), f32),
            jax.ShapeDtypeStruct((count, width), bf16),
        ),
        in_specs=[ANY] * 6,
        out_specs=(VMEM,) * 4,
        scratch_shapes=[
            pltpu.VMEM((2, count, width), bf16),
            pltpu.VMEM((2, count, width), bf16),
            pltpu.VMEM(win.shape, bf16),
            pltpu.VMEM(wout.shape, bf16),
            pltpu.SemaphoreType.DMA((6,)),
        ],
        compiler_params=LIMIT,
        cost_estimate=cost(6),
        name="experts_first",
    )(*rows, *d_rows, win, wout)


def experts_result(hidden, wout):
    _, count, units = hidden.shape
    width = wout.shape[1]

    def kernel(hidden_r, wout_r, keep_o, send_o):
        send_o[...] = dot(hidden_r[1], wout_r[...]).astype(bf16)
        keep_o[...] = dot(hidden_r[0], wout_r[...])

    return pl.pallas_call(
        kernel,
        out_shape=(
            jax.ShapeDtypeStruct((count, width), f32),
            jax.ShapeDtypeStruct((count, width), bf16),
        ),
        in_specs=[VMEM] * 2,
        out_specs=(VMEM,) * 2,
        compiler_params=LIMIT,
        cost_estimate=cost(2),
        name="experts_result",
    )(hidden, wout)


def experts_gradients(rows, d_rows, hidden, d_pre):
    width = rows[0].shape[1]
    units = hidden[0].shape[2]

    def kernel(*refs):
        row_refs, d_refs, hidden_r, d_pre_r = refs[0:4], refs[4:8], refs[8:10], refs[10:12]
        in_o, out_o = refs[12:]
        for i in range(4):
            g_in = t_dot(row_refs[i][...], d_pre_r[i // 2][i % 2])
            g_out = t_dot(hidden_r[i // 2][i % 2], d_refs[i][...])
            if i == 0:
                in_o[...] = g_in
                out_o[...] = g_out
            else:
                in_o[...] += g_in
                out_o[...] += g_out

    return pl.pallas_call(
        kernel,
        out_shape=(
            jax.ShapeDtypeStruct((width, units), f32),
            jax.ShapeDtypeStruct((units, width), f32),
        ),
        in_specs=[VMEM] * 12,
        out_specs=(VMEM,) * 2,
        compiler_params=LIMIT,
        cost_estimate=cost(10),
        name="experts_gradients",
    )(*rows, *d_rows, *hidden, *d_pre)


def block_output(returned, residual, first_t, second_t, gates):
    def kernel(held, res, first, second, gate, out):
        moe_out = gate[:, 0:1] * dot(first[...], held[...])
        moe_out = moe_out + gate[:, 1:2] * dot(second[...], held[...])
        out[...] = (res[...] + moe_out).astype(bf16)

    return pl.pallas_call(
        kernel,
        out_shape=jax.ShapeDtypeStruct(residual.shape, bf16),
        in_specs=[VMEM] * 5,
        out_specs=VMEM,
        compiler_params=LIMIT,
        cost_estimate=cost(3),
        name="block_output",
    )(returned, residual, first_t, second_t, gates)


def pack_small(packed, small):
    high = small.astype(bf16).astype(f32)
    packed[...] = jnp.zeros_like(packed)
    packed[0:12, :] = high
    packed[12:24, :] = small - high


def unpack_small(rows):
    rows = rows.astype(f32)
    return rows[0:12, :] + rows[12:24, :]


def shape_of(rows, width, dtype):
    return jax.ShapeDtypeStruct((rows, width), dtype)


def projection_gradient(normed, mixed, right, small):
    count, width = normed[0].shape
    block, first = width // 8, 2 * width // 3

    def kernel(*refs):
        normed_r, mixed_r, right_r, small_r = refs[0:4], refs[4:8], refs[8:12], refs[12]
        keep_y, send_y, keep_z = refs[13:16]
        send_z, small_o, total, packed = refs[16:19], refs[19], refs[20], refs[21]
        e_here = lax.axis_index("expert")
        last = lax.axis_index("dp") == 3
        y_here, z_here = lax.rem(e_here, 2), lax.div(e_here, 2)
        acc = None
        for i in range(4):
            left = jnp.where(last, mixed_r[i][...], normed_r[i][...])
            term = t_dot(left, right_r[i][0:count, :])
            acc = term if acc is None else acc + term
        for i in range(8):
            total[i] = acc[i * block : (i + 1) * block]
        for k in range(4):
            z_block = (z_here ^ k) * 2
            rows = slice(k * block, (k + 1) * block)
            keep_y[rows, :] = total[z_block + y_here, :, 0:first]
            send_y[rows, :] = total[z_block + 1 - y_here, :, 0:first].astype(bf16)
            for i, y in enumerate((y_here, 1 - y_here)):
                rows = slice(i * block, (i + 1) * block)
                if k == 0:
                    keep_z[rows, :] = total[z_block + y, :, first:]
                else:
                    send_z[k - 1][rows, :] = total[z_block + y, :, first:].astype(bf16)
        four = small_r[0:4, :]
        for i in range(1, 4):
            part = right_r[i][count:, :].astype(f32)
            four = four + part[0:4, :] + part[4:8, :]
        small_o[...] = jnp.zeros_like(small_o)
        for c in range(3):
            small_o[4 * c : 4 * c + 4, :] = four[:, 256 * c : 256 * c + 256]
        pack_small(packed, small_o[0:12, :])
        for k in range(3):
            send_z[k][2 * block :, :] = packed[...].astype(bf16)

    return pl.pallas_call(
        kernel,
        out_shape=(
            shape_of(4 * block, first, f32),
            shape_of(4 * block, first, bf16),
            shape_of(2 * block, width - first, f32),
        )
        + (shape_of(2 * block + 32, width - first, bf16),) * 3
        + (shape_of(16, 256, f32),),
        in_specs=[VMEM] * 13,
        out_specs=(VMEM,) * 7,
        scratch_shapes=[pltpu.VMEM((8, block, width), f32), pltpu.VMEM((32, 256), f32)],
        compiler_params=LIMIT,
        cost_estimate=cost(3),
        name="projection_gradient",
    )(*normed, *mixed, *right, small)


def middle_sums(keep_y, got_y, keep_z, got_z, small):
    block, first, rest = keep_z.shape[0] // 2, keep_y.shape[1], keep_z.shape[1]

    def kernel(keep_y, got_y, keep_z, z_1, z_2, z_3, small_r, *outs):
        own_y, send_y, own_z, send_z, small_o, packed = outs[0], outs[1:4], *outs[4:]
        for k in range(4):
            rows = slice(k * block, (k + 1) * block)
            sums = keep_y[rows, :] + got_y[rows, :].astype(f32)
            if k == 0:
                own_y[...] = sums
            else:
                send_y[k - 1][...] = sums.astype(bf16)
        sums = keep_z[...]
        small = small_r[0:12, :]
        for ref in (z_1, z_2, z_3):
            sums = sums + ref[0 : 2 * block, :].astype(f32)
            small = small + unpack_small(ref[2 * block :, :])
        own_z[...] = sums[0:block]
        send_z[0:block, :] = sums[block:].astype(bf16)
        small_o[...] = jnp.zeros_like(small_o)
        small_o[0:12, :] = small
        pack_small(packed, small)
        send_z[block:, :] = packed[...].astype(bf16)

    return pl.pallas_call(
        kernel,
        out_shape=(shape_of(block, first, f32),)
        + (shape_of(block, first, bf16),) * 3
        + (
            shape_of(block, rest, f32),
            shape_of(block + 32, rest, bf16),
            shape_of(16, 256, f32),
        ),
        in_specs=[VMEM] * 7,
        out_specs=(VMEM,) * 7,
        scratch_shapes=[pltpu.VMEM((32, 256), f32)],
        compiler_params=LIMIT,
        cost_estimate=cost(1),
        name="middle_sums",
    )(keep_y, got_y, keep_z, *got_z, small)


def last_sums(own_y, got_y, own_z, got_z, small, lookup, heads):
    block, first = own_y.shape
    rest = own_z.shape[1]
    buckets, count = lookup.shape

    def kernel(own_y, z_1, z_2, z_3, own_z, got_z, small_r, look, out, table, gain_a, gain_f, diag):
        sums = own_y[...]
        for ref in (z_1, z_2, z_3):
            sums = sums + ref[...].astype(f32)
        out[:, 0:first] = sums
        out[:, first:] = own_z[...] + got_z[0:block, :].astype(f32)
        small = small_r[0:12, :] + unpack_small(got_z[block:, :])
        for c in range(3):
            lanes = slice(256 * c, 256 * c + 256)
            gain_a[lanes] = small[4 * c + 2, :]
            gain_f[lanes] = small[4 * c + 3, :]
            for half in range(2):
                for row in range(2):
                    head = 6 * row + 2 * c + half
                    part = small[4 * c + row : 4 * c + row + 1, 128 * half : 128 * half + 128]
                    diag[head : head + 1, :] = part
        table[...] = lax.dot_general(
            diag[...],
            look[...],
            (((1,), (1,)), ((), ())),
            precision=top_precision,
            preferred_element_type=f32,
        )

    return pl.pallas_call(
        kernel,
        out_shape=(
            shape_of(block, first + rest, f32),
            shape_of(heads, buckets, f32),
            jax.ShapeDtypeStruct((first + rest,), f32),
            jax.ShapeDtypeStruct((first + rest,), f32),
        ),
        in_specs=[VMEM] * 8,
        out_specs=(VMEM,) * 4,
        scratch_shapes=[pltpu.VMEM((heads, count), f32)],
        compiler_params=LIMIT,
        cost_estimate=cost(1),
        name="last_sums",
    )(own_y, *got_y, own_z, got_z, small, lookup)


def exchange_plain(chunks):
    return lax.all_to_all(chunks, "expert", split_axis=0, concat_axis=0, tiled=True)


def spread(rows):
    x_rows = swap_x(rows)
    return [rows, swap_core(rows), x_rows, swap_core(x_rows)]


def collect(here, there):
    there = (there[0] + there[1].astype(f32)).astype(bf16)
    return here[0] + here[1].astype(f32), swap_x(there)


def total(here, from_x):
    return (here + from_x.astype(f32)).astype(bf16)


def of_members(rows):
    from_x = swap_x(rows)
    return [rows, from_x, swap_core(rows), swap_core(from_x)]


def by_projection(parts):
    from_x, passed = swap_x(parts[2]), swap_x(parts[3])
    return [parts[0], from_x, swap_core(parts[1]), swap_core(passed)]


def sum_experts(value):
    bits = 1
    while bits < lax.axis_size("expert"):
        value = value + swap(value, "expert", bits)
        bits *= 2
    return value


def reduce_projection(normed, mixed, right, small, lookup, heads):
    experts = lax.axis_size("expert")
    count = normed[0].shape[0]
    if experts != 8:
        small = small[0:4]
        for part in right[1:]:
            small = small + part[count : count + 4].astype(f32)
            small = small + part[count + 4 : count + 8].astype(f32)
        left = jnp.where(
            lax.axis_index("dp") == 3, jnp.concatenate(mixed), jnp.concatenate(normed)
        )
        right = jnp.concatenate([part[:count] for part in right])
        grad = jnp.einsum("td,te->de", left, right, preferred_element_type=f32)
        grad = lax.psum_scatter(grad, "expert", scatter_dimension=0, tiled=True)
        small = sum_experts(small)
        table = lax.dot_general(
            small[0:2].reshape(heads, lookup.shape[1]),
            lookup,
            (((1,), (1,)), ((), ())),
            precision=top_precision,
            preferred_element_type=f32,
        )
        return grad, table, small[2], small[3]
    keep_y, send_y, keep_z, *send_z, small = projection_gradient(normed, mixed, right, small)
    got_z = [swap(send_z[k], "expert", 2 * k + 2) for k in range(3)]
    got_y = swap(send_y, "expert", 1)
    own_y, *send_y, own_z, send_z, small = middle_sums(keep_y, got_y, keep_z, got_z, small)
    got_y = [swap(send_y[k], "expert", 2 * k + 2) for k in range(3)]
    got_z = swap(send_z, "expert", 1)
    return last_sums(own_y, got_y, own_z, got_z, small, lookup, heads)


def shards(
    tokens,
    attn_weights,
    gain_attn,
    gain_ffn,
    rel_table,
    expert_in,
    expert_out,
    gate_weights,
    expert_ids,
    doc_ids,
    cotangent,
):
    seqs, seq_len = doc_ids.shape
    width = tokens.shape[1]
    head_count = rel_table.shape[1]
    head_size = width // head_count
    bucket_count = rel_table.shape[0]
    experts = lax.axis_size("expert")
    token_count = tokens.shape[0]
    block_cap = 3 * seq_len // experts
    capacity = block_cap * seqs
    slots = experts * capacity
    win, wout = expert_in[0], expert_out[0]

    flat_ids = expert_ids.reshape(-1)
    pairs = flat_ids.shape[0]
    earlier = np.tril(np.ones((pairs, pairs), dtype=np.bool_), -1)
    rank = jnp.sum(
        ((flat_ids[:, None] == flat_ids[None, :]) & earlier).astype(jnp.int32), axis=1
    )
    positions = (flat_ids * capacity + rank).reshape(token_count, 2)
    slot_iota = jnp.arange(slots, dtype=jnp.int32)
    first_hit = slot_iota[:, None] == positions[None, :, 0]
    second_hit = slot_iota[:, None] == positions[None, :, 1]
    select = (first_hit | second_hit).astype(bf16)
    first_t = (slot_iota[None, :] == positions[:, 0:1]).astype(bf16)
    second_t = (slot_iota[None, :] == positions[:, 1:2]).astype(bf16)
    select_t = first_t + second_t
    gate_slot = jnp.sum(
        jnp.where(first_hit, gate_weights[None, :, 0], 0.0)
        + jnp.where(second_hit, gate_weights[None, :, 1], 0.0),
        axis=1,
    )

    by_expert = (experts, capacity, width)

    d_buffer = gate_slot[:, None] * jnp.dot(select, cotangent, preferred_element_type=f32)
    d_buffer = d_buffer.astype(bf16).reshape(by_expert)

    distance = (token_count - np.arange(token_count)) % token_count
    lookup = np.eye(bucket_count, dtype=np.float32)[
        bucket_table(seq_len, bucket_count - 1)[np.minimum(distance, seq_len - 1), 0]
    ]
    lookup = jnp.asarray((lookup * (distance < seq_len)[:, None]).T)
    bias_rows = lax.dot_general(
        rel_table,
        lookup,
        (((0,), (0,)), ((), ())),
        precision=top_precision,
        preferred_element_type=f32,
    )
    gains = jnp.stack([gain_attn, gain_ffn])
    docs = doc_ids + 4 * jnp.arange(seqs, dtype=jnp.int32)[:, None]
    docs_row = docs.astype(f32).reshape(1, -1)
    prepared = (bias_rows, gains, docs_row, select)
    pieces, offsets, d_got, prepared = gather_projections(attn_weights, d_buffer, prepared)
    bias_rows, gains, docs_row, select = prepared
    d_all = spread(d_got.reshape(slots, width))
    normed, mixed, qkv, probs, residual, buffer = attention_forward(
        pieces, offsets, tokens, gains, bias_rows, docs_row, select, head_count
    )

    got = exchange_plain(buffer.reshape(by_expert)).reshape(slots, width)
    x_rows, rows = swap_x(got), [got, swap_core(got)]
    hidden_0, d_pre_0, keep_0, send_0 = experts_first(rows, d_all[:2], win, wout)
    result_0, away_0 = experts_result(hidden_0, wout)
    x_rows, send_0, away_0 = lax.optimization_barrier((x_rows, send_0, away_0))
    rows = rows + [x_rows, swap_core(x_rows)]
    core_0, back_0 = swap_core(send_0), swap_core(away_0)
    hidden_1, d_pre_1, keep_1, send_1 = experts_first(rows[2:], d_all[2:], win, wout)
    core_1 = swap_core(send_1)
    hidden_1, d_pre_1, core_1 = lax.optimization_barrier((hidden_1, d_pre_1, core_1))
    d_rows = total(*collect((keep_0, core_0), (keep_1, core_1)))
    d_returned = exchange_plain(d_rows.reshape(by_expert)).reshape(slots, width)
    result_1, away_1 = experts_result(hidden_1, wout)
    back_1 = swap_core(away_1)
    grad_in, grad_out = experts_gradients(
        rows, d_all, (hidden_0, hidden_1), (d_pre_0, d_pre_1)
    )
    here, from_x = collect((result_0, back_0), (result_1, back_1))
    from_x, grad_in, grad_out = lax.optimization_barrier((from_x, grad_in, grad_out))
    result = total(here, from_x)
    d_returned, result, normed, mixed = lax.optimization_barrier(
        (d_returned, result, normed, mixed)
    )
    returned = exchange_plain(result.reshape(by_expert)).reshape(slots, width)
    normed, mixed = of_members(normed), of_members(mixed)

    *grads, grad_tokens, small = attention_backward(
        pieces,
        offsets,
        tokens,
        gains,
        cotangent,
        residual,
        d_returned,
        select_t,
        qkv,
        probs,
        head_count,
    )

    grads, normed, mixed = lax.optimization_barrier((grads, normed, mixed))
    right = by_projection(grads)
    right, returned = lax.optimization_barrier((right, returned))
    output = block_output(returned, residual, first_t, second_t, gate_weights)
    grad_attn, d_table, d_gain_attn, d_gain_ffn = reduce_projection(
        normed, mixed, right, small, lookup, head_count
    )
    return (
        output,
        grad_tokens,
        grad_attn,
        d_gain_attn,
        d_gain_ffn,
        d_table.T,
        grad_in[None],
        grad_out[None],
    )


def solution(mesh):
    placed = (
        P(("dp", "expert"), None),
        P(("dp", "expert"), None),
        P(),
        P(),
        P(),
        P("expert", None, "dp"),
        P("expert", "dp", None),
        P(("dp", "expert"), None),
        P(("dp", "expert"), None),
        P(("dp", "expert"), None),
        P(("dp", "expert"), None),
    )
    return jax.shard_map(
        shards,
        mesh=mesh,
        in_specs=placed,
        out_specs=(
            P(("dp", "expert"), None),
            P(("dp", "expert"), None),
            P(("dp", "expert"), None),
            P(),
            P(),
            P(),
            P("expert", None, "dp"),
            P("expert", "dp", None),
        ),
        check_vma=False,
    )
```

```python
import jax
import jax.numpy as jnp
import numpy as np
from jax import lax
from jax.experimental import pallas as pl
from jax.experimental.pallas import tpu as pltpu
from jax.sharding import PartitionSpec as P

epsilon = 1e-06
top_precision = lax.Precision.HIGHEST
f32 = jnp.float32
bf16 = jnp.bfloat16


def bucket_table(length, top_bucket):
    offset = np.arange(length)[:, None] - np.arange(length)[None, :]
    offset = np.maximum(offset, 0)
    octave = offset * 0
    for exponent in range(1, 24):
        octave = octave + (offset >= 2**exponent)
    shifted = offset >> np.maximum(octave - 2, 0)
    logbucket = 16 + 4 * (octave - 4) + (shifted & 3)
    return np.where(offset < 16, offset, np.minimum(logbucket, top_bucket))


def swap(value, axis, bits):
    size = lax.axis_size(axis)
    return lax.ppermute(value, axis, [(i, i ^ bits) for i in range(size)])


def swap_core(value):
    return swap(value, "dp", 1)


def swap_x(value):
    return swap(value, "dp", 2)


def gather_projections(block, d_buffer, prepared):
    experts = lax.axis_size("expert")
    if experts != 8:
        full = lax.all_gather(block, ("dp", "expert"), axis=0, tiled=True)
        return [full[None]], [None], exchange_plain(d_buffer), prepared
    first = [swap(block, "expert", bits) for bits in (4, 6, 2, 1)] + [swap_x(block)]
    first, prepared = lax.optimization_barrier((first, prepared))
    z_far, z_last, z_near, near_y, near_x = first
    two = jnp.stack([z_far, z_near])
    two_y = swap(two, "expert", 1)
    two_x = swap_x(two)
    last_x = swap_x(z_last)
    last_y = swap(z_last, "expert", 1)
    near_xy = swap(near_x, "expert", 1)
    two_y, last_x = lax.optimization_barrier((two_y, last_x))
    two_yx = swap_x(two_y)
    last_xy = swap(last_x, "expert", 1)
    two_x, d_buffer = lax.optimization_barrier((two_x, d_buffer))
    d_got = exchange_plain(d_buffer)
    one = jnp.stack([block, near_y, near_x])
    arrays = [one, two, two_y, two_x, two_yx]
    offsets = [
        [(0, 0), (0, 1), (2, 0)],
        [(0, 4), (0, 2)],
        [(0, 5), (0, 3)],
        [(2, 4), (2, 2)],
        [(2, 5), (2, 3)],
    ]
    rest = jnp.stack([z_last, last_x, last_y, near_xy])
    arrays = arrays + [rest, last_xy[None]]
    offsets = offsets + [[(0, 6), (2, 6), (0, 7), (2, 1)], [(2, 7)]]
    arrays = arrays + [swap_core(a) for a in arrays]
    offsets = offsets + [[(d + 1, e) for d, e in group] for group in offsets]
    return arrays, offsets, d_got, prepared


def place_projections(pieces, offsets, dense, sems):
    copies = []
    d_here, e_here = lax.axis_index("dp"), lax.axis_index("expert")
    experts = lax.axis_size("expert")
    for piece, group in zip(pieces, offsets):
        rows = piece.shape[1]
        for i in range(piece.shape[0]):
            target = dense
            if group is not None:
                block = (d_here ^ group[i][0]) * experts + (e_here ^ group[i][1])
                target = dense.at[pl.ds(pl.multiple_of(block * rows, rows), rows)]
            copies.append(pltpu.make_async_copy(piece.at[i], target, sems.at[len(copies)]))
    for copy in copies:
        copy.start()
    return copies


VMEM = pl.BlockSpec(memory_space=pltpu.VMEM)
ANY = pl.BlockSpec(memory_space=pl.ANY)
LIMIT = pltpu.CompilerParams(vmem_limit_bytes=56 * 1024 * 1024)

LESS = pltpu.CompilerParams(vmem_limit_bytes=24 * 1024 * 1024)


def held(arrays):
    return [pltpu.with_memory_space_constraint(a, pltpu.VMEM) for a in arrays]


def cost(microseconds):
    return pl.CostEstimate(
        flops=int(microseconds * 1.0e9), bytes_accessed=int(microseconds * 3.0e6), transcendentals=0
    )


def dot(a, b):
    return jnp.dot(a, b, preferred_element_type=f32)


def dot_t(a, b):
    return lax.dot_general(a, b, (((1,), (1,)), ((), ())), preferred_element_type=f32)


def t_dot(a, b):
    return lax.dot_general(a, b, (((0,), (0,)), ((), ())), preferred_element_type=f32)


def inverse_rms(values):
    return lax.rsqrt(jnp.mean(values * values, axis=-1, keepdims=True) + epsilon)


def attention_forward(
    pieces, offsets, tokens, gains, bias_rows, docs_row, select, heads
):
    count, width = tokens.shape
    slots = select.shape[0]
    blocks = sum(p.shape[0] for p in pieces)
    n = len(pieces)

    def kernel(*refs):
        piece_refs, refs = refs[:n], refs[n:]
        tok, gain, bias, drow, sel = refs[:5]
        left_o, qkv_o, probs_o, residual_o, buffer_o, dense, sems = refs[5:]
        copies = place_projections(piece_refs, offsets, dense, sems)
        x = tok[...].astype(f32)
        normed = (x * inverse_rms(x) * gain[0:1, :]).astype(bf16)
        left_o[0] = normed
        row = lax.broadcasted_iota(jnp.int32, (count, count), 0)
        col = lax.broadcasted_iota(jnp.int32, (count, count), 1)
        docs = jnp.broadcast_to(drow[...], (count, count))
        allowed = (docs == docs.T) & (col <= row)
        low_lanes = lax.broadcasted_iota(jnp.int32, (count, 128), 1) < 64
        for copy in copies:
            copy.wait()
        for i in range(3):
            qkv_o[i] = dot(normed, dense[i * width : (i + 1) * width, :]).astype(bf16)
        for pair in range(heads // 2):
            lanes = slice(128 * pair, 128 * pair + 128)
            q, k, v = qkv_o[0, :, lanes], qkv_o[1, :, lanes], qkv_o[2, :, lanes]
            out = []
            for half in range(2):
                mask = low_lanes if half == 0 else ~low_lanes
                head = 2 * pair + half
                shift = jnp.broadcast_to(bias[head : head + 1, :], (count, 128))
                shift = pltpu.roll(shift, 0, 1, stride=1, stride_axis=0)
                scores = dot_t(jnp.where(mask, q, jnp.zeros_like(q)), k) * 0.125 + shift
                scores = jnp.where(allowed, scores, -1000000000.0)
                scores = jnp.exp(scores - jnp.max(scores, axis=-1, keepdims=True))
                probs = scores * (1.0 / jnp.sum(scores, axis=-1, keepdims=True))
                probs_o[head] = probs
                out.append(dot(probs.astype(bf16), v))
            left_o[1, :, lanes] = jnp.where(low_lanes, out[0], out[1]).astype(bf16)
        residual = x + dot(left_o[1], dense[3 * width : 4 * width, :])
        residual_o[...] = residual
        moe_in = (residual * inverse_rms(residual) * gain[1:2, :]).astype(bf16)
        buffer_o[...] = dot(sel[...], moe_in).astype(bf16)

    return pl.pallas_call(
        kernel,
        out_shape=(
            jax.ShapeDtypeStruct((2, count, width), bf16),
            jax.ShapeDtypeStruct((3, count, width), bf16),
            jax.ShapeDtypeStruct((heads, count, count), f32),
            jax.ShapeDtypeStruct((count, width), f32),
            jax.ShapeDtypeStruct((slots, width), bf16),
        ),
        in_specs=[ANY] * n + [VMEM] * 5,
        out_specs=(VMEM,) * 5,
        scratch_shapes=[
            pltpu.VMEM((4 * width, width), bf16),
            pltpu.SemaphoreType.DMA((blocks,)),
        ],
        compiler_params=LIMIT,
        cost_estimate=cost(3),
        name="attention_forward",
    )(*pieces, tokens, gains, bias_rows, docs_row, select)


def attention_backward(
    pieces, offsets, tokens, gains, cotangent, residual, d_returned, select_t, qkv, probs, heads
):
    count, width = tokens.shape
    blocks = sum(p.shape[0] for p in pieces)
    n = len(pieces)

    def kernel(*refs):
        piece_refs, refs = refs[:n], refs[n:]
        tok, gain, cot, res, d_ret, sel_t, qkv_r, probs_r = refs[:8]
        outs, (d_tok_o, small_o) = refs[8:12], refs[12:14]
        dense, d_mixed_s, grads_o, packed_s, sems = refs[14:]
        d_here = lax.axis_index("dp")
        copies = place_projections(piece_refs, offsets, dense, sems)
        d_moe = dot(sel_t[...], d_ret[...])
        residual = res[...]
        r = inverse_rms(residual)
        small_o[3:4, :] = jnp.sum(d_moe * residual * r, axis=0, keepdims=True)
        m = d_moe * gain[1:2, :]
        mean = jnp.mean(m * residual, axis=-1, keepdims=True)
        d_residual = cot[...].astype(f32) + r * m - r * r * r * residual * mean
        d_tok_o[...] = d_residual
        d_attn = d_residual.astype(bf16)
        grads_o[d_here ^ 3] = d_attn
        for copy in copies:
            copy.wait()
        d_mixed_s[...] = dot_t(d_attn, dense[3 * width : 4 * width, :]).astype(bf16)
        low_lanes = lax.broadcasted_iota(jnp.int32, (count, 128), 1) < 64
        row = lax.broadcasted_iota(jnp.int32, (count, count), 0)
        col = lax.broadcasted_iota(jnp.int32, (count, count), 1)
        reverse = (row + col == count - 1).astype(f32).astype(bf16)
        for pair in range(heads // 2):
            lanes = slice(128 * pair, 128 * pair + 128)
            q, k, v = qkv_r[0, :, lanes], qkv_r[1, :, lanes], qkv_r[2, :, lanes]
            d_mix = d_mixed_s[:, lanes]
            d_q, d_k, d_v = [], [], []
            for half in range(2):
                mask = low_lanes if half == 0 else ~low_lanes
                head = 2 * pair + half
                probs = probs_r[head]
                d_probs = dot_t(jnp.where(mask, d_mix, jnp.zeros_like(d_mix)), v)
                d_v.append(t_dot(probs.astype(bf16), d_mix))
                inner = jnp.sum(probs * d_probs, axis=-1, keepdims=True)
                d_scores = (probs * (d_probs - inner)).astype(bf16)
                d_q.append(dot(d_scores, k))
                d_k.append(t_dot(d_scores, q))
                turned = pltpu.roll(dot(reverse, d_scores), 1, 1, stride=1, stride_axis=0)
                at, slot = head // 6, 128 * (head % 6)
                small_o[at : at + 1, slot : slot + 128] = jnp.sum(turned, axis=0, keepdims=True)
            grads_o[d_here ^ 0, :, lanes] = (jnp.where(low_lanes, d_q[0], d_q[1]) * 0.125).astype(bf16)
            grads_o[d_here ^ 1, :, lanes] = (jnp.where(low_lanes, d_k[0], d_k[1]) * 0.125).astype(bf16)
            grads_o[d_here ^ 2, :, lanes] = jnp.where(low_lanes, d_v[0], d_v[1]).astype(bf16)
        outs[0][...] = grads_o[0]
        d_normed = dot_t(grads_o[d_here ^ 0], dense[0:width, :])
        d_normed = d_normed + dot_t(grads_o[d_here ^ 1], dense[width : 2 * width, :])
        d_normed = d_normed + dot_t(grads_o[d_here ^ 2], dense[2 * width : 3 * width, :])
        x = tok[...].astype(f32)
        s = inverse_rms(x)
        small_o[2:3, :] = jnp.sum(d_normed * x * s, axis=0, keepdims=True)
        m = d_normed * gain[0:1, :]
        mean = jnp.mean(m * x, axis=-1, keepdims=True)
        d_tok_o[...] += s * m - s * s * s * x * mean
        small = small_o[0:4, :]
        high = small.astype(bf16).astype(f32)
        packed_s[...] = jnp.zeros_like(packed_s)
        packed_s[0:4, :] = high
        packed_s[4:8, :] = small - high
        for i in range(1, 4):
            outs[i][0:count, :] = grads_o[i]
            outs[i][count:, :] = packed_s[...].astype(bf16)

    return pl.pallas_call(
        kernel,
        out_shape=(jax.ShapeDtypeStruct((count, width), bf16),)
        + (jax.ShapeDtypeStruct((count + 16, width), bf16),) * 3
        + (
            jax.ShapeDtypeStruct((count, width), f32),
            jax.ShapeDtypeStruct((8, width), f32),
        ),
        in_specs=[ANY] * n + [VMEM] * 8,
        out_specs=(VMEM,) * 6,
        scratch_shapes=[
            pltpu.VMEM((4 * width, width), bf16),
            pltpu.VMEM((count, width), bf16),
            pltpu.VMEM((4, count, width), bf16),
            pltpu.VMEM((16, width), f32),
            pltpu.SemaphoreType.DMA((blocks,)),
        ],
        compiler_params=LIMIT,
        cost_estimate=cost(13),
        name="attention_backward",
    )(*pieces, tokens, gains, cotangent, residual, d_returned, select_t, qkv, probs)


def gelu_parts(v):
    c = 0.7978845608028654
    square = v * v
    t = jnp.tanh(c * v * (1.0 + 0.044715 * square))
    half = 0.5 * (1.0 + t)
    slope = half + 0.5 * v * (1.0 - t * t) * (c + (3.0 * 0.044715 * c) * square)
    return v * half, slope


def experts_first(rows, d_rows, win, wout):
    count, width = rows[0].shape
    units = win.shape[1]

    def kernel(*refs):
        row_refs, d_refs, (win_r, wout_r) = refs[0:2], refs[2:4], refs[4:6]
        hidden_o, d_pre_o, keep_o, send_o = refs[6:]
        for i in (1, 0):
            d_hidden = dot_t(d_refs[i][...], wout_r[...])
            pre = dot(row_refs[i][...], win_r[...])
            hidden, slope = gelu_parts(pre)
            hidden_o[i] = hidden.astype(bf16)
            d_pre = (d_hidden * slope).astype(bf16)
            d_pre_o[i] = d_pre
            d_slot = dot_t(d_pre, win_r[...])
            if i == 1:
                send_o[...] = d_slot.astype(bf16)
            else:
                keep_o[...] = d_slot

    return pl.pallas_call(
        kernel,
        out_shape=(
            jax.ShapeDtypeStruct((2, count, units), bf16),
            jax.ShapeDtypeStruct((2, count, units), bf16),
            jax.ShapeDtypeStruct((count, width), f32),
            jax.ShapeDtypeStruct((count, width), bf16),
        ),
        in_specs=[VMEM] * 6,
        out_specs=(VMEM,) * 4,
        compiler_params=LESS,
        cost_estimate=cost(6),
        name="experts_first",
    )(*held([*rows, *d_rows, win, wout]))


def experts_result(hidden, wout):
    _, count, units = hidden.shape
    width = wout.shape[1]

    def kernel(hidden_r, wout_r, keep_o, send_o):
        send_o[...] = dot(hidden_r[1], wout_r[...]).astype(bf16)
        keep_o[...] = dot(hidden_r[0], wout_r[...])

    return pl.pallas_call(
        kernel,
        out_shape=(
            jax.ShapeDtypeStruct((count, width), f32),
            jax.ShapeDtypeStruct((count, width), bf16),
        ),
        in_specs=[VMEM] * 2,
        out_specs=(VMEM,) * 2,
        compiler_params=LESS,
        cost_estimate=cost(2),
        name="experts_result",
    )(*held([hidden, wout]))


def experts_gradients(rows, d_rows, hidden, d_pre):
    width = rows[0].shape[1]
    units = hidden[0].shape[2]

    def kernel(*refs):
        row_refs, d_refs, hidden_r, d_pre_r = refs[0:4], refs[4:8], refs[8:10], refs[10:12]
        in_o, out_o = refs[12:]
        for i in range(4):
            g_in = t_dot(row_refs[i][...], d_pre_r[i // 2][i % 2])
            g_out = t_dot(hidden_r[i // 2][i % 2], d_refs[i][...])
            if i == 0:
                in_o[...] = g_in
                out_o[...] = g_out
            else:
                in_o[...] += g_in
                out_o[...] += g_out

    return pl.pallas_call(
        kernel,
        out_shape=(
            jax.ShapeDtypeStruct((width, units), f32),
            jax.ShapeDtypeStruct((units, width), f32),
        ),
        in_specs=[VMEM] * 12,
        out_specs=(VMEM,) * 2,
        compiler_params=LIMIT,
        cost_estimate=cost(10),
        name="experts_gradients",
    )(*rows, *d_rows, *hidden, *d_pre)


def block_output(returned, residual, first_t, second_t, gates):
    def kernel(held, res, first, second, gate, out):
        moe_out = gate[:, 0:1] * dot(first[...], held[...])
        moe_out = moe_out + gate[:, 1:2] * dot(second[...], held[...])
        out[...] = (res[...] + moe_out).astype(bf16)

    return pl.pallas_call(
        kernel,
        out_shape=jax.ShapeDtypeStruct(residual.shape, bf16),
        in_specs=[VMEM] * 5,
        out_specs=VMEM,
        compiler_params=LIMIT,
        cost_estimate=cost(3),
        name="block_output",
    )(returned, residual, first_t, second_t, gates)


def pack_small(packed, small):
    high = small.astype(bf16).astype(f32)
    packed[...] = jnp.zeros_like(packed)
    packed[0:12, :] = high
    packed[12:24, :] = small - high


def unpack_small(rows):
    rows = rows.astype(f32)
    return rows[0:12, :] + rows[12:24, :]


def shape_of(rows, width, dtype):
    return jax.ShapeDtypeStruct((rows, width), dtype)


def projection_gradient(left, right, small):
    _, count, width = left[0].shape
    block, first = width // 8, 2 * width // 3

    def kernel(*refs):
        left_r, right_r, small_r = refs[0:4], refs[4:8], refs[8]
        keep_y, send_y, keep_z = refs[9:12]
        send_z, small_o, total, packed = refs[12:15], refs[15], refs[16], refs[17]
        left_s, right_s = refs[18:20]
        e_here = lax.axis_index("expert")
        which = lax.div(lax.axis_index("dp"), 3)
        y_here, z_here = lax.rem(e_here, 2), lax.div(e_here, 2)
        for i in range(4):
            rows = slice(i * count, (i + 1) * count)
            left_s[rows, :] = left_r[i][which]
            right_s[rows, :] = right_r[i][0:count, :]
        acc = t_dot(left_s[...], right_s[...])
        for i in range(8):
            total[i] = acc[i * block : (i + 1) * block]
        for k in range(4):
            z_block = (z_here ^ k) * 2
            rows = slice(k * block, (k + 1) * block)
            keep_y[rows, :] = total[z_block + y_here, :, 0:first]
            send_y[rows, :] = total[z_block + 1 - y_here, :, 0:first].astype(bf16)
            for i, y in enumerate((y_here, 1 - y_here)):
                rows = slice(i * block, (i + 1) * block)
                if k == 0:
                    keep_z[rows, :] = total[z_block + y, :, first:]
                else:
                    send_z[k - 1][rows, :] = total[z_block + y, :, first:].astype(bf16)
        four = small_r[0:4, :]
        for i in range(1, 4):
            part = right_r[i][count:, :].astype(f32)
            four = four + part[0:4, :] + part[4:8, :]
        small_o[...] = jnp.zeros_like(small_o)
        for c in range(3):
            small_o[4 * c : 4 * c + 4, :] = four[:, 256 * c : 256 * c + 256]
        pack_small(packed, small_o[0:12, :])
        for k in range(3):
            send_z[k][2 * block :, :] = packed[...].astype(bf16)

    return pl.pallas_call(
        kernel,
        out_shape=(
            shape_of(4 * block, first, f32),
            shape_of(4 * block, first, bf16),
            shape_of(2 * block, width - first, f32),
        )
        + (shape_of(2 * block + 32, width - first, bf16),) * 3
        + (shape_of(16, 256, f32),),
        in_specs=[VMEM] * 9,
        out_specs=(VMEM,) * 7,
        scratch_shapes=[pltpu.VMEM((8, block, width), f32), pltpu.VMEM((32, 256), f32)]
        + [pltpu.VMEM((4 * count, width), bf16)] * 2,
        compiler_params=LESS,
        cost_estimate=cost(3),
        name="projection_gradient",
    )(*held([*left, *right, small]))


def middle_sums(keep_y, got_y, keep_z, got_z, small):
    block, first, rest = keep_z.shape[0] // 2, keep_y.shape[1], keep_z.shape[1]

    def kernel(keep_y, got_y, keep_z, z_1, z_2, z_3, small_r, *outs):
        own_y, send_y, own_z, send_z, small_o, packed = outs[0], outs[1:4], *outs[4:]
        for k in range(4):
            rows = slice(k * block, (k + 1) * block)
            sums = keep_y[rows, :] + got_y[rows, :].astype(f32)
            if k == 0:
                own_y[...] = sums
            else:
                send_y[k - 1][...] = sums.astype(bf16)
        sums = keep_z[...]
        small = small_r[0:12, :]
        for ref in (z_1, z_2, z_3):
            sums = sums + ref[0 : 2 * block, :].astype(f32)
            small = small + unpack_small(ref[2 * block :, :])
        own_z[...] = sums[0:block]
        send_z[0:block, :] = sums[block:].astype(bf16)
        small_o[...] = jnp.zeros_like(small_o)
        small_o[0:12, :] = small
        pack_small(packed, small)
        send_z[block:, :] = packed[...].astype(bf16)

    return pl.pallas_call(
        kernel,
        out_shape=(shape_of(block, first, f32),)
        + (shape_of(block, first, bf16),) * 3
        + (
            shape_of(block, rest, f32),
            shape_of(block + 32, rest, bf16),
            shape_of(16, 256, f32),
        ),
        in_specs=[VMEM] * 7,
        out_specs=(VMEM,) * 7,
        scratch_shapes=[pltpu.VMEM((32, 256), f32)],
        compiler_params=LESS,
        cost_estimate=cost(1),
        name="middle_sums",
    )(*held([keep_y, got_y, keep_z, *got_z, small]))


def last_sums(own_y, got_y, own_z, got_z, small, lookup, heads):
    block, first = own_y.shape
    rest = own_z.shape[1]
    buckets, count = lookup.shape

    def kernel(own_y, z_1, z_2, z_3, own_z, got_z, small_r, look, out, table, gain_a, gain_f, diag):
        sums = own_y[...]
        for ref in (z_1, z_2, z_3):
            sums = sums + ref[...].astype(f32)
        out[:, 0:first] = sums
        out[:, first:] = own_z[...] + got_z[0:block, :].astype(f32)
        small = small_r[0:12, :] + unpack_small(got_z[block:, :])
        for c in range(3):
            lanes = slice(256 * c, 256 * c + 256)
            gain_a[lanes] = small[4 * c + 2, :]
            gain_f[lanes] = small[4 * c + 3, :]
            for half in range(2):
                for row in range(2):
                    head = 6 * row + 2 * c + half
                    part = small[4 * c + row : 4 * c + row + 1, 128 * half : 128 * half + 128]
                    diag[head : head + 1, :] = part
        table[...] = lax.dot_general(
            diag[...],
            look[...],
            (((1,), (1,)), ((), ())),
            precision=top_precision,
            preferred_element_type=f32,
        )

    return pl.pallas_call(
        kernel,
        out_shape=(
            shape_of(block, first + rest, f32),
            shape_of(heads, buckets, f32),
            jax.ShapeDtypeStruct((first + rest,), f32),
            jax.ShapeDtypeStruct((first + rest,), f32),
        ),
        in_specs=[VMEM] * 8,
        out_specs=(VMEM,) * 4,
        scratch_shapes=[pltpu.VMEM((heads, count), f32)],
        compiler_params=LESS,
        cost_estimate=cost(1),
        name="last_sums",
    )(*held([own_y, *got_y, own_z, got_z, small, lookup]))


def exchange_plain(chunks):
    return lax.all_to_all(chunks, "expert", split_axis=0, concat_axis=0, tiled=True)


def spread(rows):
    x_rows = swap_x(rows)
    return [rows, swap_core(rows), x_rows, swap_core(x_rows)]


def collect(here, there):
    there = (there[0] + there[1].astype(f32)).astype(bf16)
    return here[0] + here[1].astype(f32), swap_x(there)


def total(here, from_x):
    return (here + from_x.astype(f32)).astype(bf16)


def by_projection(parts):
    from_x, passed = swap_x(parts[2]), swap_x(parts[3])
    return [parts[0], from_x, swap_core(parts[1]), swap_core(passed)]


def sum_experts(value):
    bits = 1
    while bits < lax.axis_size("expert"):
        value = value + swap(value, "expert", bits)
        bits *= 2
    return value


def reduce_projection(left, right, small, lookup, heads):
    experts = lax.axis_size("expert")
    count = left[0].shape[1]
    if experts != 8:
        small = small[0:4]
        for part in right[1:]:
            small = small + part[count : count + 4].astype(f32)
            small = small + part[count + 4 : count + 8].astype(f32)
        left = jnp.concatenate(left, axis=1)
        left = jnp.where(lax.axis_index("dp") == 3, left[1], left[0])
        right = jnp.concatenate([part[:count] for part in right])
        grad = jnp.einsum("td,te->de", left, right, preferred_element_type=f32)
        grad = lax.psum_scatter(grad, "expert", scatter_dimension=0, tiled=True)
        small = sum_experts(small)
        table = lax.dot_general(
            small[0:2].reshape(heads, lookup.shape[1]),
            lookup,
            (((1,), (1,)), ((), ())),
            precision=top_precision,
            preferred_element_type=f32,
        )
        return grad, table, small[2], small[3]
    keep_y, send_y, keep_z, *send_z, small = projection_gradient(left, right, small)
    got_z = [swap(send_z[k], "expert", 2 * k + 2) for k in range(3)]
    got_y = swap(send_y, "expert", 1)
    own_y, *send_y, own_z, send_z, small = middle_sums(keep_y, got_y, keep_z, got_z, small)
    got_y = [swap(send_y[k], "expert", 2 * k + 2) for k in range(3)]
    got_z = swap(send_z, "expert", 1)
    return last_sums(own_y, got_y, own_z, got_z, small, lookup, heads)


def shards(
    tokens,
    attn_weights,
    gain_attn,
    gain_ffn,
    rel_table,
    expert_in,
    expert_out,
    gate_weights,
    expert_ids,
    doc_ids,
    cotangent,
):
    seqs, seq_len = doc_ids.shape
    width = tokens.shape[1]
    head_count = rel_table.shape[1]
    head_size = width // head_count
    bucket_count = rel_table.shape[0]
    experts = lax.axis_size("expert")
    token_count = tokens.shape[0]
    block_cap = 3 * seq_len // experts
    capacity = block_cap * seqs
    slots = experts * capacity
    win, wout = expert_in[0], expert_out[0]

    flat_ids = expert_ids.reshape(-1)
    pairs = flat_ids.shape[0]
    earlier = np.tril(np.ones((pairs, pairs), dtype=np.bool_), -1)
    rank = jnp.sum(
        ((flat_ids[:, None] == flat_ids[None, :]) & earlier).astype(jnp.int32), axis=1
    )
    positions = (flat_ids * capacity + rank).reshape(token_count, 2)
    slot_iota = jnp.arange(slots, dtype=jnp.int32)
    first_hit = slot_iota[:, None] == positions[None, :, 0]
    second_hit = slot_iota[:, None] == positions[None, :, 1]
    select = (first_hit | second_hit).astype(bf16)
    first_t = (slot_iota[None, :] == positions[:, 0:1]).astype(bf16)
    second_t = (slot_iota[None, :] == positions[:, 1:2]).astype(bf16)
    select_t = first_t + second_t
    gate_slot = jnp.sum(
        jnp.where(first_hit, gate_weights[None, :, 0], 0.0)
        + jnp.where(second_hit, gate_weights[None, :, 1], 0.0),
        axis=1,
    )

    by_expert = (experts, capacity, width)

    d_buffer = gate_slot[:, None] * jnp.dot(select, cotangent, preferred_element_type=f32)
    d_buffer = d_buffer.astype(bf16).reshape(by_expert)

    distance = (token_count - np.arange(token_count)) % token_count
    lookup = np.eye(bucket_count, dtype=np.float32)[
        bucket_table(seq_len, bucket_count - 1)[np.minimum(distance, seq_len - 1), 0]
    ]
    lookup = jnp.asarray((lookup * (distance < seq_len)[:, None]).T)
    bias_rows = lax.dot_general(
        rel_table,
        lookup,
        (((0,), (0,)), ((), ())),
        precision=top_precision,
        preferred_element_type=f32,
    )
    gains = jnp.stack([gain_attn, gain_ffn])
    docs = doc_ids + 4 * jnp.arange(seqs, dtype=jnp.int32)[:, None]
    docs_row = docs.astype(f32).reshape(1, -1)
    prepared = (bias_rows, gains, docs_row, select)
    pieces, offsets, d_got, prepared = gather_projections(attn_weights, d_buffer, prepared)
    bias_rows, gains, docs_row, select = prepared
    d_all = spread(d_got.reshape(slots, width))
    left, qkv, probs, residual, buffer = attention_forward(
        pieces, offsets, tokens, gains, bias_rows, docs_row, select, head_count
    )

    got = exchange_plain(buffer.reshape(by_expert)).reshape(slots, width)
    x_rows, rows = swap_x(got), [got, swap_core(got)]
    hidden_0, d_pre_0, keep_0, send_0 = experts_first(rows, d_all[:2], win, wout)
    result_0, away_0 = experts_result(hidden_0, wout)
    x_rows, send_0, away_0 = lax.optimization_barrier((x_rows, send_0, away_0))
    rows = rows + [x_rows, swap_core(x_rows)]
    core_0, back_0 = swap_core(send_0), swap_core(away_0)
    hidden_1, d_pre_1, keep_1, send_1 = experts_first(rows[2:], d_all[2:], win, wout)
    core_1 = swap_core(send_1)
    hidden_1, d_pre_1, core_1 = lax.optimization_barrier((hidden_1, d_pre_1, core_1))
    here, from_x = collect((keep_0, core_0), (keep_1, core_1))
    prepared = (first_t, second_t, select_t)
    from_x, prepared = lax.optimization_barrier((from_x, prepared))
    first_t, second_t, select_t = prepared
    d_rows = total(here, from_x)
    result_1, away_1 = experts_result(hidden_1, wout)
    back_1 = swap_core(away_1)
    d_returned = exchange_plain(d_rows.reshape(by_expert)).reshape(slots, width)
    grad_in, grad_out = experts_gradients(
        rows, d_all, (hidden_0, hidden_1), (d_pre_0, d_pre_1)
    )
    here, from_x = collect((result_0, back_0), (result_1, back_1))
    from_x, grad_in, grad_out = lax.optimization_barrier((from_x, grad_in, grad_out))
    result = total(here, from_x)
    d_returned, result, left = lax.optimization_barrier((d_returned, result, left))
    returned = exchange_plain(result.reshape(by_expert)).reshape(slots, width)
    left_x = swap_x(left)

    *grads, grad_tokens, small = attention_backward(
        pieces,
        offsets,
        tokens,
        gains,
        cotangent,
        residual,
        d_returned,
        select_t,
        qkv,
        probs,
        head_count,
    )

    grads, left_x = lax.optimization_barrier((grads, left_x))
    left = [left, left_x, swap_core(left), swap_core(left_x)]
    right = by_projection(grads)
    right, returned = lax.optimization_barrier((right, returned))
    output = block_output(returned, residual, first_t, second_t, gate_weights)
    grad_attn, d_table, d_gain_attn, d_gain_ffn = reduce_projection(
        left, right, small, lookup, head_count
    )
    return (
        output,
        grad_tokens,
        grad_attn,
        d_gain_attn,
        d_gain_ffn,
        d_table.T,
        grad_in[None],
        grad_out[None],
    )


def solution(mesh):
    placed = (
        P(("dp", "expert"), None),
        P(("dp", "expert"), None),
        P(),
        P(),
        P(),
        P("expert", None, "dp"),
        P("expert", "dp", None),
        P(("dp", "expert"), None),
        P(("dp", "expert"), None),
        P(("dp", "expert"), None),
        P(("dp", "expert"), None),
    )
    return jax.shard_map(
        shards,
        mesh=mesh,
        in_specs=placed,
        out_specs=(
            P(("dp", "expert"), None),
            P(("dp", "expert"), None),
            P(("dp", "expert"), None),
            P(),
            P(),
            P(),
            P("expert", None, "dp"),
            P("expert", "dp", None),
        ),
        check_vma=False,
    )
```

```python
import jax
import jax.numpy as jnp
import numpy as np
from jax import lax
from jax.experimental import pallas as pl
from jax.experimental.pallas import tpu as pltpu
from jax.sharding import PartitionSpec as P

epsilon = 1e-06
top_precision = lax.Precision.HIGHEST
f32 = jnp.float32
bf16 = jnp.bfloat16


def bucket_table(length, top_bucket):
    offset = np.arange(length)[:, None] - np.arange(length)[None, :]
    offset = np.maximum(offset, 0)
    octave = offset * 0
    for exponent in range(1, 24):
        octave = octave + (offset >= 2**exponent)
    shifted = offset >> np.maximum(octave - 2, 0)
    logbucket = 16 + 4 * (octave - 4) + (shifted & 3)
    return np.where(offset < 16, offset, np.minimum(logbucket, top_bucket))


def swap(value, axis, bits):
    size = lax.axis_size(axis)
    return lax.ppermute(value, axis, [(i, i ^ bits) for i in range(size)])


def swap_core(value):
    return swap(value, "dp", 1)


def swap_x(value):
    return swap(value, "dp", 2)


def gather_projections(block, d_buffer, prepared):
    experts = lax.axis_size("expert")
    if experts != 8:
        full = lax.all_gather(block, ("dp", "expert"), axis=0, tiled=True)
        return [full[None]], [None], exchange_plain(d_buffer), prepared
    first = [swap(block, "expert", bits) for bits in (4, 6, 2, 1)] + [swap_x(block)]
    first, prepared = lax.optimization_barrier((first, prepared))
    z_far, z_last, z_near, near_y, near_x = first
    two = jnp.stack([z_far, z_near])
    two_y = swap(two, "expert", 1)
    two_x = swap_x(two)
    last_x = swap_x(z_last)
    last_y = swap(z_last, "expert", 1)
    near_xy = swap(near_x, "expert", 1)
    two_y, last_x = lax.optimization_barrier((two_y, last_x))
    two_yx = swap_x(two_y)
    last_xy = swap(last_x, "expert", 1)
    two_x, d_buffer = lax.optimization_barrier((two_x, d_buffer))
    d_got = exchange_plain(d_buffer)
    one = jnp.stack([block, near_y, near_x])
    arrays = [one, two, two_y, two_x, two_yx]
    offsets = [
        [(0, 0), (0, 1), (2, 0)],
        [(0, 4), (0, 2)],
        [(0, 5), (0, 3)],
        [(2, 4), (2, 2)],
        [(2, 5), (2, 3)],
    ]
    rest = jnp.stack([z_last, last_x, last_y, near_xy])
    arrays = arrays + [rest, last_xy[None]]
    offsets = offsets + [[(0, 6), (2, 6), (0, 7), (2, 1)], [(2, 7)]]
    arrays = arrays + [swap_core(a) for a in arrays]
    offsets = offsets + [[(d + 1, e) for d, e in group] for group in offsets]
    return arrays, offsets, d_got, prepared


def place_projections(pieces, offsets, dense, sems):
    copies = []
    d_here, e_here = lax.axis_index("dp"), lax.axis_index("expert")
    experts = lax.axis_size("expert")
    for piece, group in zip(pieces, offsets):
        rows = piece.shape[1]
        for i in range(piece.shape[0]):
            target = dense
            if group is not None:
                block = (d_here ^ group[i][0]) * experts + (e_here ^ group[i][1])
                target = dense.at[pl.ds(pl.multiple_of(block * rows, rows), rows)]
            copies.append(pltpu.make_async_copy(piece.at[i], target, sems.at[len(copies)]))
    for copy in copies:
        copy.start()
    return copies


VMEM = pl.BlockSpec(memory_space=pltpu.VMEM)
ANY = pl.BlockSpec(memory_space=pl.ANY)
LIMIT = pltpu.CompilerParams(vmem_limit_bytes=56 * 1024 * 1024)

LESS = pltpu.CompilerParams(vmem_limit_bytes=24 * 1024 * 1024)


def held(arrays):
    return [pltpu.with_memory_space_constraint(a, pltpu.VMEM) for a in arrays]


def cost(microseconds):
    return pl.CostEstimate(
        flops=int(microseconds * 1.0e9), bytes_accessed=int(microseconds * 3.0e6), transcendentals=0
    )


def dot(a, b):
    return jnp.dot(a, b, preferred_element_type=f32)


def dot_t(a, b):
    return lax.dot_general(a, b, (((1,), (1,)), ((), ())), preferred_element_type=f32)


def t_dot(a, b):
    return lax.dot_general(a, b, (((0,), (0,)), ((), ())), preferred_element_type=f32)


def inverse_rms(values):
    return lax.rsqrt(jnp.mean(values * values, axis=-1, keepdims=True) + epsilon)


def attention_forward(
    pieces, offsets, tokens, gains, bias_rows, docs_row, select, heads
):
    count, width = tokens.shape
    slots = select.shape[0]
    blocks = sum(p.shape[0] for p in pieces)
    n = len(pieces)

    def kernel(*refs):
        piece_refs, refs = refs[:n], refs[n:]
        tok, gain, bias, drow, sel = refs[:5]
        left_o, qkv_o, probs_o, residual_o, buffer_o, dense, sems = refs[5:]
        copies = place_projections(piece_refs, offsets, dense, sems)
        x = tok[...].astype(f32)
        normed = (x * inverse_rms(x) * gain[0:1, :]).astype(bf16)
        left_o[0] = normed
        row = lax.broadcasted_iota(jnp.int32, (count, count), 0)
        col = lax.broadcasted_iota(jnp.int32, (count, count), 1)
        docs = jnp.broadcast_to(drow[...], (count, count))
        allowed = (docs == docs.T) & (col <= row)
        low_lanes = lax.broadcasted_iota(jnp.int32, (count, 128), 1) < 64
        for copy in copies:
            copy.wait()
        for i in range(3):
            qkv_o[i] = dot(normed, dense[i * width : (i + 1) * width, :]).astype(bf16)
        for pair in range(heads // 2):
            lanes = slice(128 * pair, 128 * pair + 128)
            q, k, v = qkv_o[0, :, lanes], qkv_o[1, :, lanes], qkv_o[2, :, lanes]
            out = []
            for half in range(2):
                mask = low_lanes if half == 0 else ~low_lanes
                head = 2 * pair + half
                shift = jnp.broadcast_to(bias[head : head + 1, :], (count, 128))
                shift = pltpu.roll(shift, 0, 1, stride=1, stride_axis=0)
                scores = dot_t(jnp.where(mask, q, jnp.zeros_like(q)), k) * 0.125 + shift
                scores = jnp.where(allowed, scores, -1000000000.0)
                scores = jnp.exp(scores - jnp.max(scores, axis=-1, keepdims=True))
                probs = scores * (1.0 / jnp.sum(scores, axis=-1, keepdims=True))
                probs_o[head] = probs
                out.append(dot(probs.astype(bf16), v))
            left_o[1, :, lanes] = jnp.where(low_lanes, out[0], out[1]).astype(bf16)
        residual = x + dot(left_o[1], dense[3 * width : 4 * width, :])
        residual_o[...] = residual
        moe_in = (residual * inverse_rms(residual) * gain[1:2, :]).astype(bf16)
        buffer_o[...] = dot(sel[...], moe_in).astype(bf16)

    return pl.pallas_call(
        kernel,
        out_shape=(
            jax.ShapeDtypeStruct((2, count, width), bf16),
            jax.ShapeDtypeStruct((3, count, width), bf16),
            jax.ShapeDtypeStruct((heads, count, count), f32),
            jax.ShapeDtypeStruct((count, width), f32),
            jax.ShapeDtypeStruct((slots, width), bf16),
        ),
        in_specs=[ANY] * n + [VMEM] * 5,
        out_specs=(VMEM,) * 5,
        scratch_shapes=[
            pltpu.VMEM((4 * width, width), bf16),
            pltpu.SemaphoreType.DMA((blocks,)),
        ],
        compiler_params=LIMIT,
        cost_estimate=cost(3),
        name="attention_forward",
    )(*pieces, tokens, gains, bias_rows, docs_row, select)


def attention_backward(
    pieces, offsets, tokens, gains, cotangent, residual, d_returned, select_t, qkv, probs, heads
):
    count, width = tokens.shape
    blocks = sum(p.shape[0] for p in pieces)
    n = len(pieces)

    def kernel(*refs):
        piece_refs, refs = refs[:n], refs[n:]
        tok, gain, cot, res, d_ret, sel_t, qkv_r, probs_r = refs[:8]
        outs, (d_tok_o, small_o) = refs[8:12], refs[12:14]
        dense, d_mixed_s, grads_o, packed_s, sems = refs[14:]
        d_here = lax.axis_index("dp")
        copies = place_projections(piece_refs, offsets, dense, sems)
        d_moe = dot(sel_t[...], d_ret[...])
        residual = res[...]
        r = inverse_rms(residual)
        small_o[3:4, :] = jnp.sum(d_moe * residual * r, axis=0, keepdims=True)
        m = d_moe * gain[1:2, :]
        mean = jnp.mean(m * residual, axis=-1, keepdims=True)
        d_residual = cot[...].astype(f32) + r * m - r * r * r * residual * mean
        d_tok_o[...] = d_residual
        d_attn = d_residual.astype(bf16)
        grads_o[d_here ^ 3] = d_attn
        for copy in copies:
            copy.wait()
        d_mixed_s[...] = dot_t(d_attn, dense[3 * width : 4 * width, :]).astype(bf16)
        low_lanes = lax.broadcasted_iota(jnp.int32, (count, 128), 1) < 64
        row = lax.broadcasted_iota(jnp.int32, (count, count), 0)
        col = lax.broadcasted_iota(jnp.int32, (count, count), 1)
        reverse = (row + col == count - 1).astype(f32).astype(bf16)
        for pair in range(heads // 2):
            lanes = slice(128 * pair, 128 * pair + 128)
            q, k, v = qkv_r[0, :, lanes], qkv_r[1, :, lanes], qkv_r[2, :, lanes]
            d_mix = d_mixed_s[:, lanes]
            d_q, d_k, d_v = [], [], []
            for half in range(2):
                mask = low_lanes if half == 0 else ~low_lanes
                head = 2 * pair + half
                probs = probs_r[head]
                d_probs = dot_t(jnp.where(mask, d_mix, jnp.zeros_like(d_mix)), v)
                d_v.append(t_dot(probs.astype(bf16), d_mix))
                inner = jnp.sum(probs * d_probs, axis=-1, keepdims=True)
                d_scores = (probs * (d_probs - inner)).astype(bf16)
                d_q.append(dot(d_scores, k))
                d_k.append(t_dot(d_scores, q))
                turned = pltpu.roll(dot(reverse, d_scores), 1, 1, stride=1, stride_axis=0)
                at, slot = head // 6, 128 * (head % 6)
                small_o[at : at + 1, slot : slot + 128] = jnp.sum(turned, axis=0, keepdims=True)
            grads_o[d_here ^ 0, :, lanes] = (jnp.where(low_lanes, d_q[0], d_q[1]) * 0.125).astype(bf16)
            grads_o[d_here ^ 1, :, lanes] = (jnp.where(low_lanes, d_k[0], d_k[1]) * 0.125).astype(bf16)
            grads_o[d_here ^ 2, :, lanes] = jnp.where(low_lanes, d_v[0], d_v[1]).astype(bf16)
        outs[0][...] = grads_o[0]
        d_normed = dot_t(grads_o[d_here ^ 0], dense[0:width, :])
        d_normed = d_normed + dot_t(grads_o[d_here ^ 1], dense[width : 2 * width, :])
        d_normed = d_normed + dot_t(grads_o[d_here ^ 2], dense[2 * width : 3 * width, :])
        x = tok[...].astype(f32)
        s = inverse_rms(x)
        small_o[2:3, :] = jnp.sum(d_normed * x * s, axis=0, keepdims=True)
        m = d_normed * gain[0:1, :]
        mean = jnp.mean(m * x, axis=-1, keepdims=True)
        d_tok_o[...] += s * m - s * s * s * x * mean
        small = small_o[0:4, :]
        high = small.astype(bf16).astype(f32)
        packed_s[...] = jnp.zeros_like(packed_s)
        packed_s[0:4, :] = high
        packed_s[4:8, :] = small - high
        for i in range(1, 4):
            outs[i][0:count, :] = grads_o[i]
            outs[i][count:, :] = packed_s[...].astype(bf16)

    return pl.pallas_call(
        kernel,
        out_shape=(jax.ShapeDtypeStruct((count, width), bf16),)
        + (jax.ShapeDtypeStruct((count + 16, width), bf16),) * 3
        + (
            jax.ShapeDtypeStruct((count, width), f32),
            jax.ShapeDtypeStruct((8, width), f32),
        ),
        in_specs=[ANY] * n + [VMEM] * 8,
        out_specs=(VMEM,) * 6,
        scratch_shapes=[
            pltpu.VMEM((4 * width, width), bf16),
            pltpu.VMEM((count, width), bf16),
            pltpu.VMEM((4, count, width), bf16),
            pltpu.VMEM((16, width), f32),
            pltpu.SemaphoreType.DMA((blocks,)),
        ],
        compiler_params=LIMIT,
        cost_estimate=cost(13),
        name="attention_backward",
    )(*pieces, tokens, gains, cotangent, residual, d_returned, select_t, qkv, probs)


def gelu_parts(v):
    c = 0.7978845608028654
    square = v * v
    t = jnp.tanh(c * v * (1.0 + 0.044715 * square))
    half = 0.5 * (1.0 + t)
    slope = half + 0.5 * v * (1.0 - t * t) * (c + (3.0 * 0.044715 * c) * square)
    return v * half, slope


def experts_first(rows, d_rows, win, wout):
    count, width = rows[0].shape
    units = win.shape[1]

    def kernel(*refs):
        row_refs, d_refs, (win_r, wout_r) = refs[0:2], refs[2:4], refs[4:6]
        hidden_o, d_pre_o, keep_o, send_o = refs[6:]
        for i in (1, 0):
            d_hidden = dot_t(d_refs[i][...], wout_r[...])
            pre = dot(row_refs[i][...], win_r[...])
            hidden, slope = gelu_parts(pre)
            hidden_o[i] = hidden.astype(bf16)
            d_pre = (d_hidden * slope).astype(bf16)
            d_pre_o[i] = d_pre
            d_slot = dot_t(d_pre, win_r[...])
            if i == 1:
                send_o[...] = d_slot.astype(bf16)
            else:
                keep_o[...] = d_slot

    return pl.pallas_call(
        kernel,
        out_shape=(
            jax.ShapeDtypeStruct((2, count, units), bf16),
            jax.ShapeDtypeStruct((2, count, units), bf16),
            jax.ShapeDtypeStruct((count, width), f32),
            jax.ShapeDtypeStruct((count, width), bf16),
        ),
        in_specs=[VMEM] * 6,
        out_specs=(VMEM,) * 4,
        compiler_params=LESS,
        cost_estimate=cost(6),
        name="experts_first",
    )(*held([*rows, *d_rows, win, wout]))


def experts_result(hidden, wout):
    _, count, units = hidden.shape
    width = wout.shape[1]

    def kernel(hidden_r, wout_r, keep_o, send_o):
        send_o[...] = dot(hidden_r[1], wout_r[...]).astype(bf16)
        keep_o[...] = dot(hidden_r[0], wout_r[...]).astype(bf16)

    return pl.pallas_call(
        kernel,
        out_shape=(
            jax.ShapeDtypeStruct((count, width), bf16),
            jax.ShapeDtypeStruct((count, width), bf16),
        ),
        in_specs=[VMEM] * 2,
        out_specs=(VMEM,) * 2,
        compiler_params=LESS,
        cost_estimate=cost(2),
        name="experts_result",
    )(*held([hidden, wout]))


def experts_gradients(rows, d_rows, hidden, d_pre):
    width = rows[0].shape[1]
    units = hidden[0].shape[2]

    def kernel(*refs):
        row_refs, d_refs, hidden_r, d_pre_r = refs[0:4], refs[4:8], refs[8:10], refs[10:12]
        in_o, out_o = refs[12:]
        for i in range(4):
            g_in = t_dot(row_refs[i][...], d_pre_r[i // 2][i % 2])
            g_out = t_dot(hidden_r[i // 2][i % 2], d_refs[i][...])
            if i == 0:
                in_o[...] = g_in
                out_o[...] = g_out
            else:
                in_o[...] += g_in
                out_o[...] += g_out

    return pl.pallas_call(
        kernel,
        out_shape=(
            jax.ShapeDtypeStruct((width, units), f32),
            jax.ShapeDtypeStruct((units, width), f32),
        ),
        in_specs=[VMEM] * 12,
        out_specs=(VMEM,) * 2,
        compiler_params=LIMIT,
        cost_estimate=cost(10),
        name="experts_gradients",
    )(*rows, *d_rows, *hidden, *d_pre)


def block_output(returned, residual, first_t, second_t, gates):
    def kernel(held, res, first, second, gate, out):
        moe_out = gate[:, 0:1] * dot(first[...], held[...])
        moe_out = moe_out + gate[:, 1:2] * dot(second[...], held[...])
        out[...] = (res[...] + moe_out).astype(bf16)

    return pl.pallas_call(
        kernel,
        out_shape=jax.ShapeDtypeStruct(residual.shape, bf16),
        in_specs=[VMEM] * 5,
        out_specs=VMEM,
        compiler_params=LIMIT,
        cost_estimate=cost(3),
        name="block_output",
    )(returned, residual, first_t, second_t, gates)


def pack_small(packed, small):
    high = small.astype(bf16).astype(f32)
    packed[...] = jnp.zeros_like(packed)
    packed[0:12, :] = high
    packed[12:24, :] = small - high


def unpack_small(rows):
    rows = rows.astype(f32)
    return rows[0:12, :] + rows[12:24, :]


def shape_of(rows, width, dtype):
    return jax.ShapeDtypeStruct((rows, width), dtype)


def projection_gradient(left, right, small):
    _, count, width = left[0].shape
    block, first = width // 8, 2 * width // 3

    def kernel(*refs):
        left_r, right_r, small_r = refs[0:4], refs[4:8], refs[8]
        keep_y, send_y, keep_z = refs[9:12]
        send_z, small_o, total, packed = refs[12:15], refs[15], refs[16], refs[17]
        left_s, right_s = refs[18:20]
        e_here = lax.axis_index("expert")
        which = lax.div(lax.axis_index("dp"), 3)
        y_here, z_here = lax.rem(e_here, 2), lax.div(e_here, 2)
        for i in range(4):
            rows = slice(i * count, (i + 1) * count)
            left_s[rows, :] = left_r[i][which]
            right_s[rows, :] = right_r[i][0:count, :]
        acc = t_dot(left_s[...], right_s[...])
        for i in range(8):
            total[i] = acc[i * block : (i + 1) * block]
        for k in range(4):
            z_block = (z_here ^ k) * 2
            rows = slice(k * block, (k + 1) * block)
            keep_y[rows, :] = total[z_block + y_here, :, 0:first]
            send_y[rows, :] = total[z_block + 1 - y_here, :, 0:first].astype(bf16)
            for i, y in enumerate((y_here, 1 - y_here)):
                rows = slice(i * block, (i + 1) * block)
                if k == 0:
                    keep_z[rows, :] = total[z_block + y, :, first:]
                else:
                    send_z[k - 1][rows, :] = total[z_block + y, :, first:].astype(bf16)
        four = small_r[0:4, :]
        for i in range(1, 4):
            part = right_r[i][count:, :].astype(f32)
            four = four + part[0:4, :] + part[4:8, :]
        small_o[...] = jnp.zeros_like(small_o)
        for c in range(3):
            small_o[4 * c : 4 * c + 4, :] = four[:, 256 * c : 256 * c + 256]
        pack_small(packed, small_o[0:12, :])
        for k in range(3):
            send_z[k][2 * block :, :] = packed[...].astype(bf16)

    return pl.pallas_call(
        kernel,
        out_shape=(
            shape_of(4 * block, first, f32),
            shape_of(4 * block, first, bf16),
            shape_of(2 * block, width - first, f32),
        )
        + (shape_of(2 * block + 32, width - first, bf16),) * 3
        + (shape_of(16, 256, f32),),
        in_specs=[VMEM] * 9,
        out_specs=(VMEM,) * 7,
        scratch_shapes=[pltpu.VMEM((8, block, width), f32), pltpu.VMEM((32, 256), f32)]
        + [pltpu.VMEM((4 * count, width), bf16)] * 2,
        compiler_params=LESS,
        cost_estimate=cost(3),
        name="projection_gradient",
    )(*held([*left, *right, small]))


def middle_sums(keep_y, got_y, keep_z, got_z, small):
    block, first, rest = keep_z.shape[0] // 2, keep_y.shape[1], keep_z.shape[1]

    def kernel(keep_y, got_y, keep_z, z_1, z_2, z_3, small_r, *outs):
        own_y, send_y, own_z, send_z, small_o, packed = outs[0], outs[1:4], *outs[4:]
        for k in range(4):
            rows = slice(k * block, (k + 1) * block)
            sums = keep_y[rows, :] + got_y[rows, :].astype(f32)
            if k == 0:
                own_y[...] = sums
            else:
                send_y[k - 1][...] = sums.astype(bf16)
        sums = keep_z[...]
        small = small_r[0:12, :]
        for ref in (z_1, z_2, z_3):
            sums = sums + ref[0 : 2 * block, :].astype(f32)
            small = small + unpack_small(ref[2 * block :, :])
        own_z[...] = sums[0:block]
        send_z[0:block, :] = sums[block:].astype(bf16)
        small_o[...] = jnp.zeros_like(small_o)
        small_o[0:12, :] = small
        pack_small(packed, small)
        send_z[block:, :] = packed[...].astype(bf16)

    return pl.pallas_call(
        kernel,
        out_shape=(shape_of(block, first, f32),)
        + (shape_of(block, first, bf16),) * 3
        + (
            shape_of(block, rest, f32),
            shape_of(block + 32, rest, bf16),
            shape_of(16, 256, f32),
        ),
        in_specs=[VMEM] * 7,
        out_specs=(VMEM,) * 7,
        scratch_shapes=[pltpu.VMEM((32, 256), f32)],
        compiler_params=LESS,
        cost_estimate=cost(1),
        name="middle_sums",
    )(*held([keep_y, got_y, keep_z, *got_z, small]))


def last_sums(own_y, got_y, own_z, got_z, small, lookup, heads):
    block, first = own_y.shape
    rest = own_z.shape[1]
    buckets, count = lookup.shape

    def kernel(own_y, z_1, z_2, z_3, own_z, got_z, small_r, look, out, table, gain_a, gain_f, diag):
        sums = own_y[...]
        for ref in (z_1, z_2, z_3):
            sums = sums + ref[...].astype(f32)
        out[:, 0:first] = sums
        out[:, first:] = own_z[...] + got_z[0:block, :].astype(f32)
        small = small_r[0:12, :] + unpack_small(got_z[block:, :])
        for c in range(3):
            lanes = slice(256 * c, 256 * c + 256)
            gain_a[lanes] = small[4 * c + 2, :]
            gain_f[lanes] = small[4 * c + 3, :]
            for half in range(2):
                for row in range(2):
                    head = 6 * row + 2 * c + half
                    part = small[4 * c + row : 4 * c + row + 1, 128 * half : 128 * half + 128]
                    diag[head : head + 1, :] = part
        table[...] = lax.dot_general(
            diag[...],
            look[...],
            (((1,), (1,)), ((), ())),
            precision=top_precision,
            preferred_element_type=f32,
        )

    return pl.pallas_call(
        kernel,
        out_shape=(
            shape_of(block, first + rest, f32),
            shape_of(heads, buckets, f32),
            jax.ShapeDtypeStruct((first + rest,), f32),
            jax.ShapeDtypeStruct((first + rest,), f32),
        ),
        in_specs=[VMEM] * 8,
        out_specs=(VMEM,) * 4,
        scratch_shapes=[pltpu.VMEM((heads, count), f32)],
        compiler_params=LESS,
        cost_estimate=cost(1),
        name="last_sums",
    )(*held([own_y, *got_y, own_z, got_z, small, lookup]))


def exchange_plain(chunks):
    return lax.all_to_all(chunks, "expert", split_axis=0, concat_axis=0, tiled=True)


def spread(rows):
    x_rows = swap_x(rows)
    return [rows, swap_core(rows), x_rows, swap_core(x_rows)]


def collect(here, there):
    there = (there[0].astype(f32) + there[1].astype(f32)).astype(bf16)
    return here[0].astype(f32) + here[1].astype(f32), swap_x(there)


def total(here, from_x):
    return (here + from_x.astype(f32)).astype(bf16)


def by_projection(parts):
    from_x, passed = swap_x(parts[2]), swap_x(parts[3])
    return [parts[0], from_x, swap_core(parts[1]), swap_core(passed)]


def sum_experts(value):
    bits = 1
    while bits < lax.axis_size("expert"):
        value = value + swap(value, "expert", bits)
        bits *= 2
    return value


def reduce_projection(left, right, small, lookup, heads):
    experts = lax.axis_size("expert")
    count = left[0].shape[1]
    if experts != 8:
        small = small[0:4]
        for part in right[1:]:
            small = small + part[count : count + 4].astype(f32)
            small = small + part[count + 4 : count + 8].astype(f32)
        left = jnp.concatenate(left, axis=1)
        left = jnp.where(lax.axis_index("dp") == 3, left[1], left[0])
        right = jnp.concatenate([part[:count] for part in right])
        grad = jnp.einsum("td,te->de", left, right, preferred_element_type=f32)
        grad = lax.psum_scatter(grad, "expert", scatter_dimension=0, tiled=True)
        small = sum_experts(small)
        table = lax.dot_general(
            small[0:2].reshape(heads, lookup.shape[1]),
            lookup,
            (((1,), (1,)), ((), ())),
            precision=top_precision,
            preferred_element_type=f32,
        )
        return grad, table, small[2], small[3]
    keep_y, send_y, keep_z, *send_z, small = projection_gradient(left, right, small)
    got_z = [swap(send_z[k], "expert", 2 * k + 2) for k in range(3)]
    got_y = swap(send_y, "expert", 1)
    own_y, *send_y, own_z, send_z, small = middle_sums(keep_y, got_y, keep_z, got_z, small)
    got_y = [swap(send_y[k], "expert", 2 * k + 2) for k in range(3)]
    got_z = swap(send_z, "expert", 1)
    return last_sums(own_y, got_y, own_z, got_z, small, lookup, heads)


def shards(
    tokens,
    attn_weights,
    gain_attn,
    gain_ffn,
    rel_table,
    expert_in,
    expert_out,
    gate_weights,
    expert_ids,
    doc_ids,
    cotangent,
):
    seqs, seq_len = doc_ids.shape
    width = tokens.shape[1]
    head_count = rel_table.shape[1]
    head_size = width // head_count
    bucket_count = rel_table.shape[0]
    experts = lax.axis_size("expert")
    token_count = tokens.shape[0]
    block_cap = 3 * seq_len // experts
    capacity = block_cap * seqs
    slots = experts * capacity
    win, wout = expert_in[0], expert_out[0]

    flat_ids = expert_ids.reshape(-1)
    pairs = flat_ids.shape[0]
    earlier = np.tril(np.ones((pairs, pairs), dtype=np.bool_), -1)
    rank = jnp.sum(
        ((flat_ids[:, None] == flat_ids[None, :]) & earlier).astype(jnp.int32), axis=1
    )
    positions = (flat_ids * capacity + rank).reshape(token_count, 2)
    slot_iota = jnp.arange(slots, dtype=jnp.int32)
    first_hit = slot_iota[:, None] == positions[None, :, 0]
    second_hit = slot_iota[:, None] == positions[None, :, 1]
    select = (first_hit | second_hit).astype(bf16)
    first_t = (slot_iota[None, :] == positions[:, 0:1]).astype(bf16)
    second_t = (slot_iota[None, :] == positions[:, 1:2]).astype(bf16)
    select_t = first_t + second_t
    gate_slot = jnp.sum(
        jnp.where(first_hit, gate_weights[None, :, 0], 0.0)
        + jnp.where(second_hit, gate_weights[None, :, 1], 0.0),
        axis=1,
    )

    by_expert = (experts, capacity, width)

    d_buffer = gate_slot[:, None] * jnp.dot(select, cotangent, preferred_element_type=f32)
    d_buffer = d_buffer.astype(bf16).reshape(by_expert)

    distance = (token_count - np.arange(token_count)) % token_count
    lookup = np.eye(bucket_count, dtype=np.float32)[
        bucket_table(seq_len, bucket_count - 1)[np.minimum(distance, seq_len - 1), 0]
    ]
    lookup = jnp.asarray((lookup * (distance < seq_len)[:, None]).T)
    bias_rows = lax.dot_general(
        rel_table,
        lookup,
        (((0,), (0,)), ((), ())),
        precision=top_precision,
        preferred_element_type=f32,
    )
    gains = jnp.stack([gain_attn, gain_ffn])
    docs = doc_ids + 4 * jnp.arange(seqs, dtype=jnp.int32)[:, None]
    docs_row = docs.astype(f32).reshape(1, -1)
    prepared = (bias_rows, gains, docs_row, select)
    pieces, offsets, d_got, prepared = gather_projections(attn_weights, d_buffer, prepared)
    bias_rows, gains, docs_row, select = prepared
    d_all = spread(d_got.reshape(slots, width))
    left, qkv, probs, residual, buffer = attention_forward(
        pieces, offsets, tokens, gains, bias_rows, docs_row, select, head_count
    )

    got = exchange_plain(buffer.reshape(by_expert)).reshape(slots, width)
    x_rows, rows = swap_x(got), [got, swap_core(got)]
    hidden_0, d_pre_0, keep_0, send_0 = experts_first(rows, d_all[:2], win, wout)
    result_0, away_0 = experts_result(hidden_0, wout)
    x_rows, send_0, away_0, left = lax.optimization_barrier((x_rows, send_0, away_0, left))
    left_x = swap_x(left)
    rows = rows + [x_rows, swap_core(x_rows)]
    core_0, back_0 = swap_core(send_0), swap_core(away_0)
    hidden_1, d_pre_1, keep_1, send_1 = experts_first(rows[2:], d_all[2:], win, wout)
    core_1 = swap_core(send_1)
    hidden_1, d_pre_1, core_1 = lax.optimization_barrier((hidden_1, d_pre_1, core_1))
    here, from_x = collect((keep_0, core_0), (keep_1, core_1))
    prepared = (first_t, second_t, select_t)
    from_x, prepared = lax.optimization_barrier((from_x, prepared))
    first_t, second_t, select_t = prepared
    d_rows = total(here, from_x)
    result_1, away_1 = experts_result(hidden_1, wout)
    back_1 = swap_core(away_1)
    d_returned = exchange_plain(d_rows.reshape(by_expert)).reshape(slots, width)
    grad_in, grad_out = experts_gradients(
        rows, d_all, (hidden_0, hidden_1), (d_pre_0, d_pre_1)
    )
    here, from_x = collect((result_0, back_0), (result_1, back_1))
    from_x, grad_in, grad_out = lax.optimization_barrier((from_x, grad_in, grad_out))
    result = total(here, from_x)
    d_returned, result, left = lax.optimization_barrier((d_returned, result, left))
    returned = exchange_plain(result.reshape(by_expert)).reshape(slots, width)

    *grads, grad_tokens, small = attention_backward(
        pieces,
        offsets,
        tokens,
        gains,
        cotangent,
        residual,
        d_returned,
        select_t,
        qkv,
        probs,
        head_count,
    )

    grads, left_x = lax.optimization_barrier((grads, left_x))
    left = [left, left_x, swap_core(left), swap_core(left_x)]
    right = by_projection(grads)
    right, returned = lax.optimization_barrier((right, returned))
    output = block_output(returned, residual, first_t, second_t, gate_weights)
    grad_attn, d_table, d_gain_attn, d_gain_ffn = reduce_projection(
        left, right, small, lookup, head_count
    )
    return (
        output,
        grad_tokens,
        grad_attn,
        d_gain_attn,
        d_gain_ffn,
        d_table.T,
        grad_in[None],
        grad_out[None],
    )


def solution(mesh):
    placed = (
        P(("dp", "expert"), None),
        P(("dp", "expert"), None),
        P(),
        P(),
        P(),
        P("expert", None, "dp"),
        P("expert", "dp", None),
        P(("dp", "expert"), None),
        P(("dp", "expert"), None),
        P(("dp", "expert"), None),
        P(("dp", "expert"), None),
    )
    return jax.shard_map(
        shards,
        mesh=mesh,
        in_specs=placed,
        out_specs=(
            P(("dp", "expert"), None),
            P(("dp", "expert"), None),
            P(("dp", "expert"), None),
            P(),
            P(),
            P(),
            P("expert", None, "dp"),
            P("expert", "dp", None),
        ),
        check_vma=False,
    )
```

```python
import jax
import jax.numpy as jnp
import numpy as np
from jax import lax
from jax.experimental import pallas as pl
from jax.experimental.pallas import tpu as pltpu
from jax.sharding import PartitionSpec as P

epsilon = 1e-06
top_precision = lax.Precision.HIGHEST
f32 = jnp.float32
bf16 = jnp.bfloat16


def bucket_table(length, top_bucket):
    offset = np.arange(length)[:, None] - np.arange(length)[None, :]
    offset = np.maximum(offset, 0)
    octave = offset * 0
    for exponent in range(1, 24):
        octave = octave + (offset >= 2**exponent)
    shifted = offset >> np.maximum(octave - 2, 0)
    logbucket = 16 + 4 * (octave - 4) + (shifted & 3)
    return np.where(offset < 16, offset, np.minimum(logbucket, top_bucket))


def swap(value, axis, bits):
    size = lax.axis_size(axis)
    return lax.ppermute(value, axis, [(i, i ^ bits) for i in range(size)])


def swap_core(value):
    return swap(value, "dp", 1)


def swap_x(value):
    return swap(value, "dp", 2)


def gather_projections(block, d_buffer, prepared):
    experts = lax.axis_size("expert")
    if experts != 8:
        full = lax.all_gather(block, ("dp", "expert"), axis=0, tiled=True)
        return [full[None]], [None], exchange_plain(d_buffer), prepared
    first = [swap(block, "expert", bits) for bits in (4, 6, 2, 1)] + [swap_x(block)]
    first, prepared = lax.optimization_barrier((first, prepared))
    z_far, z_last, z_near, near_y, near_x = first
    two = jnp.stack([z_far, z_near])
    two_y = swap(two, "expert", 1)
    two_x = swap_x(two)
    last_x = swap_x(z_last)
    last_y = swap(z_last, "expert", 1)
    near_xy = swap(near_x, "expert", 1)
    two_y, last_x = lax.optimization_barrier((two_y, last_x))
    two_yx = swap_x(two_y)
    last_xy = swap(last_x, "expert", 1)
    two_x, d_buffer = lax.optimization_barrier((two_x, d_buffer))
    d_got = exchange_plain(d_buffer)
    one = jnp.stack([block, near_y, near_x])
    arrays = [one, two, two_y, two_x, two_yx]
    offsets = [
        [(0, 0), (0, 1), (2, 0)],
        [(0, 4), (0, 2)],
        [(0, 5), (0, 3)],
        [(2, 4), (2, 2)],
        [(2, 5), (2, 3)],
    ]
    rest = jnp.stack([z_last, last_x, last_y, near_xy])
    arrays = arrays + [rest, last_xy[None]]
    offsets = offsets + [[(0, 6), (2, 6), (0, 7), (2, 1)], [(2, 7)]]
    arrays = arrays + [swap_core(a) for a in arrays]
    offsets = offsets + [[(d + 1, e) for d, e in group] for group in offsets]
    return arrays, offsets, d_got, prepared


def place_projections(pieces, offsets, dense, sems):
    copies = []
    d_here, e_here = lax.axis_index("dp"), lax.axis_index("expert")
    experts = lax.axis_size("expert")
    for piece, group in zip(pieces, offsets):
        rows = piece.shape[1]
        for i in range(piece.shape[0]):
            target = dense
            if group is not None:
                block = (d_here ^ group[i][0]) * experts + (e_here ^ group[i][1])
                target = dense.at[pl.ds(pl.multiple_of(block * rows, rows), rows)]
            copies.append(pltpu.make_async_copy(piece.at[i], target, sems.at[len(copies)]))
    for copy in copies:
        copy.start()
    return copies


VMEM = pl.BlockSpec(memory_space=pltpu.VMEM)
ANY = pl.BlockSpec(memory_space=pl.ANY)
LIMIT = pltpu.CompilerParams(vmem_limit_bytes=56 * 1024 * 1024)

LESS = pltpu.CompilerParams(vmem_limit_bytes=24 * 1024 * 1024)


def held(arrays):
    return [pltpu.with_memory_space_constraint(a, pltpu.VMEM) for a in arrays]


def cost(microseconds):
    return pl.CostEstimate(
        flops=int(microseconds * 1.0e9), bytes_accessed=int(microseconds * 3.0e6), transcendentals=0
    )


def dot(a, b):
    return jnp.dot(a, b, preferred_element_type=f32)


def dot_t(a, b):
    return lax.dot_general(a, b, (((1,), (1,)), ((), ())), preferred_element_type=f32)


def t_dot(a, b):
    return lax.dot_general(a, b, (((0,), (0,)), ((), ())), preferred_element_type=f32)


def inverse_rms(values):
    return lax.rsqrt(jnp.mean(values * values, axis=-1, keepdims=True) + epsilon)


def attention_forward(
    pieces, offsets, tokens, gains, bias_rows, docs_row, select, heads
):
    count, width = tokens.shape
    slots = select.shape[0]
    blocks = sum(p.shape[0] for p in pieces)
    n = len(pieces)

    def kernel(*refs):
        piece_refs, refs = refs[:n], refs[n:]
        tok, gain, bias, drow, sel = refs[:5]
        left_o, qkv_o, probs_o, residual_o, buffer_o, dense, sems = refs[5:]
        copies = place_projections(piece_refs, offsets, dense, sems)
        x = tok[...].astype(f32)
        normed = (x * inverse_rms(x) * gain[0:1, :]).astype(bf16)
        left_o[0] = normed
        row = lax.broadcasted_iota(jnp.int32, (count, count), 0)
        col = lax.broadcasted_iota(jnp.int32, (count, count), 1)
        docs = jnp.broadcast_to(drow[...], (count, count))
        allowed = (docs == docs.T) & (col <= row)
        low_lanes = lax.broadcasted_iota(jnp.int32, (count, 128), 1) < 64
        for copy in copies:
            copy.wait()
        for i in range(3):
            qkv_o[i] = dot(normed, dense[i * width : (i + 1) * width, :]).astype(bf16)
        for pair in range(heads // 2):
            lanes = slice(128 * pair, 128 * pair + 128)
            q, k, v = qkv_o[0, :, lanes], qkv_o[1, :, lanes], qkv_o[2, :, lanes]
            out = []
            for half in range(2):
                mask = low_lanes if half == 0 else ~low_lanes
                head = 2 * pair + half
                shift = jnp.broadcast_to(bias[head : head + 1, :], (count, 128))
                shift = pltpu.roll(shift, 0, 1, stride=1, stride_axis=0)
                scores = dot_t(jnp.where(mask, q, jnp.zeros_like(q)), k) * 0.125 + shift
                scores = jnp.where(allowed, scores, -1000000000.0)
                scores = jnp.exp(scores - jnp.max(scores, axis=-1, keepdims=True))
                probs = scores * (1.0 / jnp.sum(scores, axis=-1, keepdims=True))
                probs_o[head] = probs
                out.append(dot(probs.astype(bf16), v))
            left_o[1, :, lanes] = jnp.where(low_lanes, out[0], out[1]).astype(bf16)
        residual = x + dot(left_o[1], dense[3 * width : 4 * width, :])
        residual_o[...] = residual
        moe_in = (residual * inverse_rms(residual) * gain[1:2, :]).astype(bf16)
        buffer_o[...] = dot(sel[...], moe_in).astype(bf16)

    return pl.pallas_call(
        kernel,
        out_shape=(
            jax.ShapeDtypeStruct((2, count, width), bf16),
            jax.ShapeDtypeStruct((3, count, width), bf16),
            jax.ShapeDtypeStruct((heads, count, count), f32),
            jax.ShapeDtypeStruct((count, width), f32),
            jax.ShapeDtypeStruct((slots, width), bf16),
        ),
        in_specs=[ANY] * n + [VMEM] * 5,
        out_specs=(VMEM,) * 5,
        scratch_shapes=[
            pltpu.VMEM((4 * width, width), bf16),
            pltpu.SemaphoreType.DMA((blocks,)),
        ],
        compiler_params=LIMIT,
        cost_estimate=cost(3),
        name="attention_forward",
    )(*pieces, tokens, gains, bias_rows, docs_row, select)


def attention_backward(
    pieces, offsets, tokens, gains, cotangent, residual, d_returned, select_t, qkv, probs, heads
):
    count, width = tokens.shape
    blocks = sum(p.shape[0] for p in pieces)
    n = len(pieces)

    def kernel(*refs):
        piece_refs, refs = refs[:n], refs[n:]
        tok, gain, cot, res, d_ret, sel_t, qkv_r, probs_r = refs[:8]
        outs, (d_tok_o, small_o) = refs[8:12], refs[12:14]
        dense, d_mixed_s, grads_o, packed_s, sems = refs[14:]
        d_here = lax.axis_index("dp")
        copies = place_projections(piece_refs, offsets, dense, sems)
        d_moe = dot(sel_t[...], d_ret[...])
        residual = res[...]
        r = inverse_rms(residual)
        small_o[3:4, :] = jnp.sum(d_moe * residual * r, axis=0, keepdims=True)
        m = d_moe * gain[1:2, :]
        mean = jnp.mean(m * residual, axis=-1, keepdims=True)
        d_residual = cot[...].astype(f32) + r * m - r * r * r * residual * mean
        d_tok_o[...] = d_residual
        d_attn = d_residual.astype(bf16)
        grads_o[d_here ^ 3] = d_attn
        for copy in copies:
            copy.wait()
        d_mixed_s[...] = dot_t(d_attn, dense[3 * width : 4 * width, :]).astype(bf16)
        low_lanes = lax.broadcasted_iota(jnp.int32, (count, 128), 1) < 64
        row = lax.broadcasted_iota(jnp.int32, (count, count), 0)
        col = lax.broadcasted_iota(jnp.int32, (count, count), 1)
        reverse = (row + col == count - 1).astype(f32).astype(bf16)
        for pair in range(heads // 2):
            lanes = slice(128 * pair, 128 * pair + 128)
            q, k, v = qkv_r[0, :, lanes], qkv_r[1, :, lanes], qkv_r[2, :, lanes]
            d_mix = d_mixed_s[:, lanes]
            d_q, d_k, d_v = [], [], []
            for half in range(2):
                mask = low_lanes if half == 0 else ~low_lanes
                head = 2 * pair + half
                probs = probs_r[head]
                d_probs = dot_t(jnp.where(mask, d_mix, jnp.zeros_like(d_mix)), v)
                d_v.append(t_dot(probs.astype(bf16), d_mix))
                inner = jnp.sum(probs * d_probs, axis=-1, keepdims=True)
                d_scores = (probs * (d_probs - inner)).astype(bf16)
                d_q.append(dot(d_scores, k))
                d_k.append(t_dot(d_scores, q))
                turned = pltpu.roll(dot(reverse, d_scores), 1, 1, stride=1, stride_axis=0)
                at, slot = head // 6, 128 * (head % 6)
                small_o[at : at + 1, slot : slot + 128] = jnp.sum(turned, axis=0, keepdims=True)
            grads_o[d_here ^ 0, :, lanes] = (jnp.where(low_lanes, d_q[0], d_q[1]) * 0.125).astype(bf16)
            grads_o[d_here ^ 1, :, lanes] = (jnp.where(low_lanes, d_k[0], d_k[1]) * 0.125).astype(bf16)
            grads_o[d_here ^ 2, :, lanes] = jnp.where(low_lanes, d_v[0], d_v[1]).astype(bf16)
        outs[0][...] = grads_o[0]
        d_normed = dot_t(grads_o[d_here ^ 0], dense[0:width, :])
        d_normed = d_normed + dot_t(grads_o[d_here ^ 1], dense[width : 2 * width, :])
        d_normed = d_normed + dot_t(grads_o[d_here ^ 2], dense[2 * width : 3 * width, :])
        x = tok[...].astype(f32)
        s = inverse_rms(x)
        small_o[2:3, :] = jnp.sum(d_normed * x * s, axis=0, keepdims=True)
        m = d_normed * gain[0:1, :]
        mean = jnp.mean(m * x, axis=-1, keepdims=True)
        d_tok_o[...] += s * m - s * s * s * x * mean
        small = small_o[0:4, :]
        high = small.astype(bf16).astype(f32)
        packed_s[...] = jnp.zeros_like(packed_s)
        packed_s[0:4, :] = high
        packed_s[4:8, :] = small - high
        for i in range(1, 4):
            outs[i][0:count, :] = grads_o[i]
            outs[i][count:, :] = packed_s[...].astype(bf16)

    return pl.pallas_call(
        kernel,
        out_shape=(jax.ShapeDtypeStruct((count, width), bf16),)
        + (jax.ShapeDtypeStruct((count + 16, width), bf16),) * 3
        + (
            jax.ShapeDtypeStruct((count, width), f32),
            jax.ShapeDtypeStruct((8, width), f32),
        ),
        in_specs=[ANY] * n + [VMEM] * 8,
        out_specs=(VMEM,) * 6,
        scratch_shapes=[
            pltpu.VMEM((4 * width, width), bf16),
            pltpu.VMEM((count, width), bf16),
            pltpu.VMEM((4, count, width), bf16),
            pltpu.VMEM((16, width), f32),
            pltpu.SemaphoreType.DMA((blocks,)),
        ],
        compiler_params=LIMIT,
        cost_estimate=cost(13),
        name="attention_backward",
    )(*pieces, tokens, gains, cotangent, residual, d_returned, select_t, qkv, probs)


def gelu_parts(v):
    c = 0.7978845608028654
    square = v * v
    t = jnp.tanh(c * v * (1.0 + 0.044715 * square))
    half = 0.5 * (1.0 + t)
    slope = half + 0.5 * v * (1.0 - t * t) * (c + (3.0 * 0.044715 * c) * square)
    return v * half, slope


def experts_first(rows, d_rows, win, wout):
    count, width = rows[0].shape
    units = win.shape[1]

    def kernel(*refs):
        row_refs, d_refs, (win_r, wout_r) = refs[0:2], refs[2:4], refs[4:6]
        hidden_o, d_pre_o, keep_o, send_o = refs[6:]
        for i in (1, 0):
            d_hidden = dot_t(d_refs[i][...], wout_r[...])
            pre = dot(row_refs[i][...], win_r[...])
            hidden, slope = gelu_parts(pre)
            hidden_o[i] = hidden.astype(bf16)
            d_pre = (d_hidden * slope).astype(bf16)
            d_pre_o[i] = d_pre
            d_slot = dot_t(d_pre, win_r[...])
            if i == 1:
                send_o[...] = d_slot.astype(bf16)
            else:
                keep_o[...] = d_slot

    return pl.pallas_call(
        kernel,
        out_shape=(
            jax.ShapeDtypeStruct((2, count, units), bf16),
            jax.ShapeDtypeStruct((2, count, units), bf16),
            jax.ShapeDtypeStruct((count, width), f32),
            jax.ShapeDtypeStruct((count, width), bf16),
        ),
        in_specs=[VMEM] * 6,
        out_specs=(VMEM,) * 4,
        compiler_params=LESS,
        cost_estimate=cost(6),
        name="experts_first",
    )(*held([*rows, *d_rows, win, wout]))


def experts_result(hidden, wout):
    _, count, units = hidden.shape
    width = wout.shape[1]

    def kernel(hidden_r, wout_r, keep_o, send_o):
        send_o[...] = dot(hidden_r[1], wout_r[...]).astype(bf16)
        keep_o[...] = dot(hidden_r[0], wout_r[...]).astype(bf16)

    return pl.pallas_call(
        kernel,
        out_shape=(
            jax.ShapeDtypeStruct((count, width), bf16),
            jax.ShapeDtypeStruct((count, width), bf16),
        ),
        in_specs=[VMEM] * 2,
        out_specs=(VMEM,) * 2,
        compiler_params=LESS,
        cost_estimate=cost(2),
        name="experts_result",
    )(*held([hidden, wout]))


def experts_gradients(rows, d_rows, hidden, d_pre):
    width = rows[0].shape[1]
    units = hidden[0].shape[2]

    def kernel(*refs):
        row_refs, d_refs, hidden_r, d_pre_r = refs[0:4], refs[4:8], refs[8:10], refs[10:12]
        in_o, out_o = refs[12:]
        for i in range(4):
            g_in = t_dot(row_refs[i][...], d_pre_r[i // 2][i % 2])
            g_out = t_dot(hidden_r[i // 2][i % 2], d_refs[i][...])
            if i == 0:
                in_o[...] = g_in
                out_o[...] = g_out
            else:
                in_o[...] += g_in
                out_o[...] += g_out

    return pl.pallas_call(
        kernel,
        out_shape=(
            jax.ShapeDtypeStruct((width, units), f32),
            jax.ShapeDtypeStruct((units, width), f32),
        ),
        in_specs=[VMEM] * 12,
        out_specs=(VMEM,) * 2,
        compiler_params=LIMIT,
        cost_estimate=cost(16),
        name="experts_gradients",
    )(*rows, *d_rows, *hidden, *d_pre)


def block_output(returned, residual, first_t, second_t, gates):
    def kernel(held, res, first, second, gate, out):
        moe_out = gate[:, 0:1] * dot(first[...], held[...])
        moe_out = moe_out + gate[:, 1:2] * dot(second[...], held[...])
        out[...] = (res[...] + moe_out).astype(bf16)

    return pl.pallas_call(
        kernel,
        out_shape=jax.ShapeDtypeStruct(residual.shape, bf16),
        in_specs=[VMEM] * 5,
        out_specs=VMEM,
        compiler_params=LIMIT,
        cost_estimate=cost(3),
        name="block_output",
    )(returned, residual, first_t, second_t, gates)


def pack_small(packed, small):
    high = small.astype(bf16).astype(f32)
    packed[...] = jnp.zeros_like(packed)
    packed[0:12, :] = high
    packed[12:24, :] = small - high


def unpack_small(rows):
    rows = rows.astype(f32)
    return rows[0:12, :] + rows[12:24, :]


def shape_of(rows, width, dtype):
    return jax.ShapeDtypeStruct((rows, width), dtype)


def projection_gradient(left, right, small):
    _, count, width = left[0].shape
    block, first = width // 8, 2 * width // 3

    def kernel(*refs):
        left_r, right_r, small_r = refs[0:4], refs[4:8], refs[8]
        keep_y, send_y, keep_z = refs[9:12]
        send_z, small_o, total, packed = refs[12:15], refs[15], refs[16], refs[17]
        left_s, right_s = refs[18:20]
        e_here = lax.axis_index("expert")
        which = lax.div(lax.axis_index("dp"), 3)
        y_here, z_here = lax.rem(e_here, 2), lax.div(e_here, 2)
        for i in range(4):
            rows = slice(i * count, (i + 1) * count)
            left_s[rows, :] = left_r[i][which]
            right_s[rows, :] = right_r[i][0:count, :]
        acc = t_dot(left_s[...], right_s[...])
        for i in range(8):
            total[i] = acc[i * block : (i + 1) * block]
        for k in range(4):
            z_block = (z_here ^ k) * 2
            rows = slice(k * block, (k + 1) * block)
            keep_y[rows, :] = total[z_block + y_here, :, 0:first]
            send_y[rows, :] = total[z_block + 1 - y_here, :, 0:first].astype(bf16)
            for i, y in enumerate((y_here, 1 - y_here)):
                rows = slice(i * block, (i + 1) * block)
                if k == 0:
                    keep_z[rows, :] = total[z_block + y, :, first:]
                else:
                    send_z[k - 1][rows, :] = total[z_block + y, :, first:].astype(bf16)
        four = small_r[0:4, :]
        for i in range(1, 4):
            part = right_r[i][count:, :].astype(f32)
            four = four + part[0:4, :] + part[4:8, :]
        small_o[...] = jnp.zeros_like(small_o)
        for c in range(3):
            small_o[4 * c : 4 * c + 4, :] = four[:, 256 * c : 256 * c + 256]
        pack_small(packed, small_o[0:12, :])
        for k in range(3):
            send_z[k][2 * block :, :] = packed[...].astype(bf16)

    return pl.pallas_call(
        kernel,
        out_shape=(
            shape_of(4 * block, first, f32),
            shape_of(4 * block, first, bf16),
            shape_of(2 * block, width - first, f32),
        )
        + (shape_of(2 * block + 32, width - first, bf16),) * 3
        + (shape_of(16, 256, f32),),
        in_specs=[VMEM] * 9,
        out_specs=(VMEM,) * 7,
        scratch_shapes=[pltpu.VMEM((8, block, width), f32), pltpu.VMEM((32, 256), f32)]
        + [pltpu.VMEM((4 * count, width), bf16)] * 2,
        compiler_params=LESS,
        cost_estimate=cost(3),
        name="projection_gradient",
    )(*held([*left, *right, small]))


def middle_sums(keep_y, got_y, keep_z, got_z, small):
    block, first, rest = keep_z.shape[0] // 2, keep_y.shape[1], keep_z.shape[1]

    def kernel(keep_y, got_y, keep_z, z_1, z_2, z_3, small_r, *outs):
        own_y, send_y, own_z, send_z, small_o, packed = outs[0], outs[1:4], *outs[4:]
        for k in range(4):
            rows = slice(k * block, (k + 1) * block)
            sums = keep_y[rows, :] + got_y[rows, :].astype(f32)
            if k == 0:
                own_y[...] = sums
            else:
                send_y[k - 1][...] = sums.astype(bf16)
        sums = keep_z[...]
        small = small_r[0:12, :]
        for ref in (z_1, z_2, z_3):
            sums = sums + ref[0 : 2 * block, :].astype(f32)
            small = small + unpack_small(ref[2 * block :, :])
        own_z[...] = sums[0:block]
        send_z[0:block, :] = sums[block:].astype(bf16)
        small_o[...] = jnp.zeros_like(small_o)
        small_o[0:12, :] = small
        pack_small(packed, small)
        send_z[block:, :] = packed[...].astype(bf16)

    return pl.pallas_call(
        kernel,
        out_shape=(shape_of(block, first, f32),)
        + (shape_of(block, first, bf16),) * 3
        + (
            shape_of(block, rest, f32),
            shape_of(block + 32, rest, bf16),
            shape_of(16, 256, f32),
        ),
        in_specs=[VMEM] * 7,
        out_specs=(VMEM,) * 7,
        scratch_shapes=[pltpu.VMEM((32, 256), f32)],
        compiler_params=LESS,
        cost_estimate=cost(1),
        name="middle_sums",
    )(*held([keep_y, got_y, keep_z, *got_z, small]))


def last_sums(own_y, got_y, own_z, got_z, small, lookup, heads):
    block, first = own_y.shape
    rest = own_z.shape[1]
    buckets, count = lookup.shape

    def kernel(own_y, z_1, z_2, z_3, own_z, got_z, small_r, look, out, table, gain_a, gain_f, diag):
        sums = own_y[...]
        for ref in (z_1, z_2, z_3):
            sums = sums + ref[...].astype(f32)
        out[:, 0:first] = sums
        out[:, first:] = own_z[...] + got_z[0:block, :].astype(f32)
        small = small_r[0:12, :] + unpack_small(got_z[block:, :])
        for c in range(3):
            lanes = slice(256 * c, 256 * c + 256)
            gain_a[lanes] = small[4 * c + 2, :]
            gain_f[lanes] = small[4 * c + 3, :]
            for half in range(2):
                for row in range(2):
                    head = 6 * row + 2 * c + half
                    part = small[4 * c + row : 4 * c + row + 1, 128 * half : 128 * half + 128]
                    diag[head : head + 1, :] = part
        table[...] = lax.dot_general(
            diag[...],
            look[...],
            (((1,), (1,)), ((), ())),
            precision=top_precision,
            preferred_element_type=f32,
        )

    return pl.pallas_call(
        kernel,
        out_shape=(
            shape_of(block, first + rest, f32),
            shape_of(heads, buckets, f32),
            jax.ShapeDtypeStruct((first + rest,), f32),
            jax.ShapeDtypeStruct((first + rest,), f32),
        ),
        in_specs=[VMEM] * 8,
        out_specs=(VMEM,) * 4,
        scratch_shapes=[pltpu.VMEM((heads, count), f32)],
        compiler_params=LESS,
        cost_estimate=cost(1),
        name="last_sums",
    )(*held([own_y, *got_y, own_z, got_z, small, lookup]))


def exchange_plain(chunks):
    return lax.all_to_all(chunks, "expert", split_axis=0, concat_axis=0, tiled=True)


def spread(rows):
    x_rows = swap_x(rows)
    return [rows, swap_core(rows), x_rows, swap_core(x_rows)]


def collect(here, there):
    there = (there[0].astype(f32) + there[1].astype(f32)).astype(bf16)
    return here[0].astype(f32) + here[1].astype(f32), swap_x(there)


def total(here, from_x):
    return (here + from_x.astype(f32)).astype(bf16)


def by_projection(parts):
    from_x, passed = swap_x(parts[2]), swap_x(parts[3])
    return [parts[0], from_x, swap_core(parts[1]), swap_core(passed)]


def sum_experts(value):
    bits = 1
    while bits < lax.axis_size("expert"):
        value = value + swap(value, "expert", bits)
        bits *= 2
    return value


def reduce_projection(left, right, small, lookup, heads):
    experts = lax.axis_size("expert")
    count = left[0].shape[1]
    if experts != 8:
        small = small[0:4]
        for part in right[1:]:
            small = small + part[count : count + 4].astype(f32)
            small = small + part[count + 4 : count + 8].astype(f32)
        left = jnp.concatenate(left, axis=1)
        left = jnp.where(lax.axis_index("dp") == 3, left[1], left[0])
        right = jnp.concatenate([part[:count] for part in right])
        grad = jnp.einsum("td,te->de", left, right, preferred_element_type=f32)
        grad = lax.psum_scatter(grad, "expert", scatter_dimension=0, tiled=True)
        small = sum_experts(small)
        table = lax.dot_general(
            small[0:2].reshape(heads, lookup.shape[1]),
            lookup,
            (((1,), (1,)), ((), ())),
            precision=top_precision,
            preferred_element_type=f32,
        )
        return grad, table, small[2], small[3]
    keep_y, send_y, keep_z, *send_z, small = projection_gradient(left, right, small)
    got_z = [swap(send_z[k], "expert", 2 * k + 2) for k in range(3)]
    got_y = swap(send_y, "expert", 1)
    own_y, *send_y, own_z, send_z, small = middle_sums(keep_y, got_y, keep_z, got_z, small)
    got_y = [swap(send_y[k], "expert", 2 * k + 2) for k in range(3)]
    got_z = swap(send_z, "expert", 1)
    return last_sums(own_y, got_y, own_z, got_z, small, lookup, heads)


def shards(
    tokens,
    attn_weights,
    gain_attn,
    gain_ffn,
    rel_table,
    expert_in,
    expert_out,
    gate_weights,
    expert_ids,
    doc_ids,
    cotangent,
):
    seqs, seq_len = doc_ids.shape
    width = tokens.shape[1]
    head_count = rel_table.shape[1]
    head_size = width // head_count
    bucket_count = rel_table.shape[0]
    experts = lax.axis_size("expert")
    token_count = tokens.shape[0]
    block_cap = 3 * seq_len // experts
    capacity = block_cap * seqs
    slots = experts * capacity
    win, wout = expert_in[0], expert_out[0]

    flat_ids = expert_ids.reshape(-1)
    pairs = flat_ids.shape[0]
    earlier = np.tril(np.ones((pairs, pairs), dtype=np.bool_), -1)
    rank = jnp.sum(
        ((flat_ids[:, None] == flat_ids[None, :]) & earlier).astype(jnp.int32), axis=1
    )
    positions = (flat_ids * capacity + rank).reshape(token_count, 2)
    slot_iota = jnp.arange(slots, dtype=jnp.int32)
    first_hit = slot_iota[:, None] == positions[None, :, 0]
    second_hit = slot_iota[:, None] == positions[None, :, 1]
    select = (first_hit | second_hit).astype(bf16)
    first_t = (slot_iota[None, :] == positions[:, 0:1]).astype(bf16)
    second_t = (slot_iota[None, :] == positions[:, 1:2]).astype(bf16)
    select_t = first_t + second_t
    gate_slot = jnp.sum(
        jnp.where(first_hit, gate_weights[None, :, 0], 0.0)
        + jnp.where(second_hit, gate_weights[None, :, 1], 0.0),
        axis=1,
    )

    by_expert = (experts, capacity, width)

    d_buffer = gate_slot[:, None] * jnp.dot(select, cotangent, preferred_element_type=f32)
    d_buffer = d_buffer.astype(bf16).reshape(by_expert)

    distance = (token_count - np.arange(token_count)) % token_count
    lookup = np.eye(bucket_count, dtype=np.float32)[
        bucket_table(seq_len, bucket_count - 1)[np.minimum(distance, seq_len - 1), 0]
    ]
    lookup = jnp.asarray((lookup * (distance < seq_len)[:, None]).T)
    bias_rows = lax.dot_general(
        rel_table,
        lookup,
        (((0,), (0,)), ((), ())),
        precision=top_precision,
        preferred_element_type=f32,
    )
    gains = jnp.stack([gain_attn, gain_ffn])
    docs = doc_ids + 4 * jnp.arange(seqs, dtype=jnp.int32)[:, None]
    docs_row = docs.astype(f32).reshape(1, -1)
    prepared = (bias_rows, gains, docs_row, select)
    pieces, offsets, d_got, prepared = gather_projections(attn_weights, d_buffer, prepared)
    bias_rows, gains, docs_row, select = prepared
    d_all = spread(d_got.reshape(slots, width))
    left, qkv, probs, residual, buffer = attention_forward(
        pieces, offsets, tokens, gains, bias_rows, docs_row, select, head_count
    )

    got = exchange_plain(buffer.reshape(by_expert)).reshape(slots, width)
    x_rows, rows = swap_x(got), [got, swap_core(got)]
    hidden_0, d_pre_0, keep_0, send_0 = experts_first(rows, d_all[:2], win, wout)
    result_0, away_0 = experts_result(hidden_0, wout)
    x_rows, send_0, away_0, left = lax.optimization_barrier((x_rows, send_0, away_0, left))
    left_x = swap_x(left)
    rows = rows + [x_rows, swap_core(x_rows)]
    core_0, back_0 = swap_core(send_0), swap_core(away_0)
    hidden_1, d_pre_1, keep_1, send_1 = experts_first(rows[2:], d_all[2:], win, wout)
    core_1 = swap_core(send_1)
    hidden_1, d_pre_1, core_1 = lax.optimization_barrier((hidden_1, d_pre_1, core_1))
    here, from_x = collect((keep_0, core_0), (keep_1, core_1))
    prepared = (first_t, second_t, select_t)
    from_x, prepared = lax.optimization_barrier((from_x, prepared))
    first_t, second_t, select_t = prepared
    d_rows = total(here, from_x)
    result_1, away_1 = experts_result(hidden_1, wout)
    back_1 = swap_core(away_1)
    d_returned = exchange_plain(d_rows.reshape(by_expert)).reshape(slots, width)
    grad_in, grad_out = experts_gradients(
        rows, d_all, (hidden_0, hidden_1), (d_pre_0, d_pre_1)
    )
    here, from_x = collect((result_0, back_0), (result_1, back_1))
    from_x, grad_in, grad_out = lax.optimization_barrier((from_x, grad_in, grad_out))
    result = total(here, from_x)
    d_returned, result, left = lax.optimization_barrier((d_returned, result, left))
    returned = exchange_plain(result.reshape(by_expert)).reshape(slots, width)

    *grads, grad_tokens, small = attention_backward(
        pieces,
        offsets,
        tokens,
        gains,
        cotangent,
        residual,
        d_returned,
        select_t,
        qkv,
        probs,
        head_count,
    )

    grads, left_x = lax.optimization_barrier((grads, left_x))
    left = [left, left_x, swap_core(left), swap_core(left_x)]
    right = by_projection(grads)
    right, returned = lax.optimization_barrier((right, returned))
    output = block_output(returned, residual, first_t, second_t, gate_weights)
    grad_attn, d_table, d_gain_attn, d_gain_ffn = reduce_projection(
        left, right, small, lookup, head_count
    )
    return (
        output,
        grad_tokens,
        grad_attn,
        d_gain_attn,
        d_gain_ffn,
        d_table.T,
        grad_in[None],
        grad_out[None],
    )


def solution(mesh):
    placed = (
        P(("dp", "expert"), None),
        P(("dp", "expert"), None),
        P(),
        P(),
        P(),
        P("expert", None, "dp"),
        P("expert", "dp", None),
        P(("dp", "expert"), None),
        P(("dp", "expert"), None),
        P(("dp", "expert"), None),
        P(("dp", "expert"), None),
    )
    return jax.shard_map(
        shards,
        mesh=mesh,
        in_specs=placed,
        out_specs=(
            P(("dp", "expert"), None),
            P(("dp", "expert"), None),
            P(("dp", "expert"), None),
            P(),
            P(),
            P(),
            P("expert", None, "dp"),
            P("expert", "dp", None),
        ),
        check_vma=False,
    )
```
